256 devices in a mesh: comp: 8 (over x, z_lo), row: 32 (over y, z_hi, core).
Axes of the slice: x: 4, y: 4, z: 8 (z_hi: 4, z_lo: 2; z = z_hi * 2 + z_lo), core: 2. Of those that a mesh axis runs over, the one named last changes fastest.
Arguments:
- baseline_uvw: float32 [3, 65536], P(None, 'row'), may hold values from -8000 to 8000
- sky_positions: float32 [2, 8192], P(None, 'comp'), may hold values from -0.03 to 0.03
- fluxes: float32 [8192], P('comp'), may hold values from 0.5 to 5
- clusters: int32 [8192], P('comp'), may hold values from 0 to 63
- stations: int32 [2, 65536], P(None, 'row'), may hold values from 0 to 511
- station_gains: float32 [512, 512], P('row'), may hold values from -4.2 to 4.2
- gain_step: float32 [512, 512], P('row'), may hold values from -1.8 to 1.8
- observed_vis: float32 [2, 4, 65536], P(None, None, 'row'), may hold values from -3072 to 3072
Outputs:
- new_fluxes: float32 [8192], P('comp')
The draws below stay inside these ranges and needn't reach their ends.
Inputs may be any that keep to these rules, and one draw needn't show every extreme that they name: stations[0, r] and stations[1, r] name the two stations of row r.
All inputs are finite; a program needn't handle non-finite values.
Results may differ from the reference program's by a relative error of at most 0.011.
Values sent between devices are 32-bit elements; how exact they have to be, the bound alone decides.
No kernel may reach another device: no remote copies, remote signals or barrier semaphores. Data moves between devices by JAX's collectives and lax.ppermute only.
A program may use at most 128 MiB of HBM per device.

```python
import math
import jax
import jax.numpy as jnp
from jax import lax

S = 512
C = 64
F = 4
ROWS = 65536
COMPONENTS = 8192


def set_ends(values, key, low, largest):
    longest = values.shape.index(max(values.shape))
    spots = []
    for shift in (0, 1):
        where = [jax.random.randint(jax.random.fold_in(key, axis), (), 0, length) for axis, length in enumerate(values.shape)]
        where[longest] = (where[longest] + shift) % values.shape[longest]
        spots.append(tuple(where))
    return values.at[spots[0]].set(low).at[spots[1]].set(largest)


def levels(own_key, extent, shards, low, largest):
    level, own = 1.0, jax.random.fold_in(own_key, 6)
    for dim, blocks in shards:
        heights = jnp.exp(jax.random.uniform(jax.random.fold_in(own, dim), (blocks,), jnp.float32, low / len(shards), largest / len(shards)))
        level = level * jnp.repeat(heights, extent[dim] // blocks).reshape([-1 if axis == dim else 1 for axis in range(len(extent))])
    return level


def gaussian(own_key, shape, scale, limit, split=(), held_as=jnp.bfloat16):
    values = scale * jax.random.normal(own_key, shape, jnp.float32)
    if split:
        values = values * levels(own_key, shape, split, -0.22, 0.18)
    return jnp.clip(values, -limit, limit).astype(held_as)


def setup_inputs(seed: int = 0) -> dict:
    arg_keys = jax.random.split(jax.random.key(seed), 9)
    baseline_uvw = gaussian(arg_keys[0], (3, ROWS), 2000.0, 8000.0, ((1, 32),), jnp.float32)
    sky_positions = jnp.clip(jax.random.uniform(arg_keys[1], (2, COMPONENTS), jnp.float32, -0.03, 0.03) * levels(arg_keys[1], (2, COMPONENTS), ((1, 8),), -0.4, 0.0), -0.03, 0.03)
    fluxes = jnp.clip(jnp.exp(math.log(5.0) - 2.3025851 * jax.random.uniform(arg_keys[2], (COMPONENTS,), jnp.float32) ** levels(arg_keys[2], (COMPONENTS,), ((0, 8),), -0.2, 0.2)), 0.5, 5.0)
    clusters = set_ends(jax.random.randint(arg_keys[3], (COMPONENTS,), 0, C), jax.random.fold_in(arg_keys[3], 1), 0, C - 1).astype(jnp.int32)
    stations = set_ends(jax.random.randint(arg_keys[4], (2, ROWS), 0, S), jax.random.fold_in(arg_keys[4], 1), 0, S - 1).astype(jnp.int32)
    station_gains = gaussian(arg_keys[5], (S, 2 * F * C), 0.7, 4.2, ((0, 32),), jnp.float32)
    gain_step = gaussian(arg_keys[6], (S, 2 * F * C), 0.3, 1.8, ((0, 32),), jnp.float32)
    observed_vis = gaussian(arg_keys[7], (2, F, ROWS), 512.0, 3072.0, ((2, 32),), jnp.float32)
    return {"baseline_uvw": baseline_uvw, "sky_positions": sky_positions, "fluxes": fluxes, "clusters": clusters, "stations": stations, "station_gains": station_gains, "gain_step": gain_step, "observed_vis": observed_vis}


TWO_PI = 2.0 * math.pi

def channel_scale(channel):
    return TWO_PI * (1.0 + 0.125 * channel)

def phase_tables(east_west, north_south, vertical, sky_east, sky_north, depth_term):
    base = east_west[:, None] * sky_east[None, :] + north_south[:, None] * sky_north[None, :] + vertical[:, None] * depth_term[None, :]
    cosines = []
    sines = []
    for channel in range(F):
        angle = base * channel_scale(channel)
        cosines.append(jnp.cos(angle).astype(jnp.bfloat16))
        sines.append(jnp.sin(angle).astype(jnp.bfloat16))
    return (jnp.concatenate(cosines, axis=0), jnp.concatenate(sines, axis=0))

def station_products(gain_table, first_station, second_station):
    row_count = first_station.shape[0]
    first_gain = jnp.take(gain_table, first_station, axis=0).reshape(row_count, 2, F, C)
    second_gain = jnp.take(gain_table, second_station, axis=0).reshape(row_count, 2, F, C)
    gain_re = first_gain[:, 0] * second_gain[:, 0] + first_gain[:, 1] * second_gain[:, 1]
    gain_im = first_gain[:, 1] * second_gain[:, 0] - first_gain[:, 0] * second_gain[:, 1]
    gain_re = jnp.transpose(gain_re, (1, 0, 2)).reshape(F * row_count, C)
    gain_im = jnp.transpose(gain_im, (1, 0, 2)).reshape(F * row_count, C)
    return (gain_re, gain_im)

def reference(baseline_uvw, sky_positions, fluxes, clusters, stations, station_gains, gain_step, observed_vis):
    gain_table = station_gains + gain_step
    sky_east = sky_positions[0]
    sky_north = sky_positions[1]
    depth_term = jnp.sqrt(1.0 - sky_east * sky_east - sky_north * sky_north) - 1.0
    cluster_ids = jnp.arange(C, dtype=jnp.int32)
    sky_hot = clusters[:, None] == cluster_ids[None, :]
    flux_table = jnp.where(sky_hot, fluxes[:, None], jnp.float32(0.0)).astype(jnp.bfloat16)
    block_rows = min(2048, ROWS)
    block_count = ROWS // block_rows
    dims = (((0,), (0,)), ((), ()))

    def step(totals, block_index):
        scores, curvature = totals
        first_row = block_index * block_rows
        coords = lax.dynamic_slice_in_dim(baseline_uvw, first_row, block_rows, 1)
        pair = lax.dynamic_slice_in_dim(stations, first_row, block_rows, 1)
        cos_tab, sin_tab = phase_tables(coords[0], coords[1], coords[2], sky_east, sky_north, depth_term)
        gain_re, gain_im = station_products(gain_table, pair[0], pair[1])
        pred_re = jnp.dot(cos_tab, flux_table, preferred_element_type=jnp.float32)
        pred_im = -jnp.dot(sin_tab, flux_table, preferred_element_type=jnp.float32)
        model_re = lax.optimization_barrier(jnp.sum(gain_re * pred_re - gain_im * pred_im, axis=1))
        model_im = lax.optimization_barrier(jnp.sum(gain_re * pred_im + gain_im * pred_re, axis=1))
        observed = lax.dynamic_slice_in_dim(observed_vis, first_row, block_rows, 2).reshape(2, F * block_rows)
        resid_re = (observed[0] - model_re)[:, None]
        resid_im = (observed[1] - model_im)[:, None]
        weight_re = (resid_re * gain_re + resid_im * gain_im).astype(jnp.bfloat16)
        weight_im = (resid_im * gain_re - resid_re * gain_im).astype(jnp.bfloat16)
        scores = scores + (lax.dot_general(cos_tab, weight_re, dims, preferred_element_type=jnp.float32) - lax.dot_general(sin_tab, weight_im, dims, preferred_element_type=jnp.float32))
        curvature = curvature + lax.optimization_barrier(jnp.sum(gain_re * gain_re + gain_im * gain_im, axis=0))
        return ((scores, curvature), None)
    start_totals = (jnp.zeros((COMPONENTS, C), jnp.float32), jnp.zeros((C,), jnp.float32))
    (scores, curvature), unused = lax.scan(step, start_totals, jnp.arange(block_count, dtype=jnp.int32))
    numerator = lax.optimization_barrier(jnp.sum(jnp.where(sky_hot, scores, jnp.float32(0.0)), axis=1))
    curvature_k = lax.optimization_barrier(jnp.sum(jnp.where(sky_hot, curvature[None, :], jnp.float32(0.0)), axis=1))
    return fluxes + numerator / curvature_k
```

```python
import functools
import math

import jax
import jax.numpy as jnp
import numpy as np
from jax import lax
from jax.experimental import pallas as pl
from jax.experimental.pallas import tpu as pltpu
from jax.sharding import PartitionSpec as P

C = 64
F = 4
BLOCK = 256
WIDE = 2 * F * BLOCK
CHUNK = 256
TILE = 16
GROUPS = (3, 5)
MIB = 1 << 20
F32 = jnp.float32
BF16 = jnp.bfloat16


def unit_circle_fit():
    y = 0.5 * np.cos(np.pi * (np.arange(400) + 0.5) / 400)
    even = np.polynomial.polynomial.polyfit(y * y, np.cos(0.5 * np.pi * y), 3)
    odd = np.polynomial.polynomial.polyfit(y * y, np.sin(0.5 * np.pi * y) / y, 3)
    return [float(np.float32(v)) for v in even], [float(np.float32(v)) for v in odd]


EVEN, ODD = unit_circle_fit()
ROUND = 12582912.0


def split3(x):
    high = x.astype(BF16).astype(F32)
    rest = x - high
    mid = rest.astype(BF16).astype(F32)
    return high, mid, rest - mid


def left_terms(x):
    h, m, l = split3(x)
    return [h, h, m, h, l, m, m, l]


def right_terms(x):
    h, m, l = split3(x)
    return [h, m, h, l, h, m, l, m]


def stack_terms(terms):
    pad = jnp.zeros((8, terms[0].shape[1]), F32)
    return jnp.concatenate(terms + [pad], axis=0)


def phases(eighth):
    y = eighth - ((eighth + ROUND) - ROUND)
    y2 = y * y
    c = EVEN[0] + y2 * (EVEN[1] + y2 * (EVEN[2] + y2 * EVEN[3]))
    s = y * (ODD[0] + y2 * (ODD[1] + y2 * (ODD[2] + y2 * ODD[3])))

    def double(c, s):
        c2 = c + c
        return c2 * c - 1.0, c2 * s

    c, s = double(c, s)
    c1, s1 = double(c, s)
    c, s = double(c1, s1)
    c, s = double(c, s)
    c8, s8 = double(c, s)
    c9, s9 = c8 * c1 - s8 * s1, s8 * c1 + c8 * s1
    t = c1 + c1
    c10, s10 = t * c9 - c8, t * s9 - s8
    c11, s11 = t * c10 - c9, t * s10 - s9
    return (c8, c9, c10, c11, s8, s9, s10, s11)


def table_kernel(sky_ref, flux_ref, clus_ref, uvw_ref, *rest):
    table_ref, pred_ref, left, hot = rest[-4:]
    comps = sky_ref.shape[1]

    @pl.when(pl.program_id(0) == 0)
    def _():
        east, north = sky_ref[0:1, :], sky_ref[1:2, :]
        depth = jnp.sqrt(1.0 - east * east - north * north) - 1.0
        place = jnp.concatenate([east, north, depth], axis=0)
        left[...] = jnp.transpose(stack_terms(left_terms(place))).astype(BF16)
        ids = lax.broadcasted_iota(jnp.int32, (C, comps), 0)
        hot[...] = jnp.where(ids == clus_ref[...], flux_ref[...], 0.0).astype(BF16)

    right = stack_terms(right_terms(uvw_ref[...] * 0.125)).astype(BF16)

    def matmul(chunk):
        at = pl.ds(chunk * CHUNK, CHUNK)
        part = jnp.dot(hot[:, at], table_ref[at, :], preferred_element_type=F32)
        if chunk == 0:
            pred_ref[...] = part
        else:
            pred_ref[...] += part

    for chunk in range(comps // CHUNK):
        base = jnp.dot(
            left[pl.ds(chunk * CHUNK, CHUNK), :], right, preferred_element_type=F32
        )
        for tile in range(CHUNK // TILE):
            values = phases(base[tile * TILE : (tile + 1) * TILE, :])
            for j, value in enumerate(values):
                table_ref[
                    pl.ds(chunk * CHUNK + tile * TILE, TILE), pl.ds(j * BLOCK, BLOCK)
                ] = value.astype(BF16)
        if chunk:
            matmul(chunk - 1)
    matmul(comps // CHUNK - 1)


def make_tables(first, count, sky, fluxes, clusters, uvw, after):
    comps = sky.shape[1]
    whole = lambda i: (0, 0)
    return pl.pallas_call(
        table_kernel,
        grid=(count,),
        in_specs=[
            pl.BlockSpec((2, comps), whole),
            pl.BlockSpec((1, comps), whole),
            pl.BlockSpec((1, comps), whole),
            pl.BlockSpec((3, BLOCK), lambda i: (0, i + first)),
        ]
        + [pl.BlockSpec(memory_space=pl.ANY)] * len(after),
        out_specs=[
            pl.BlockSpec((comps, WIDE), lambda i: (0, i)),
            pl.BlockSpec((C, WIDE), lambda i: (0, i)),
        ],
        out_shape=[
            jax.ShapeDtypeStruct((comps, count * WIDE), BF16),
            jax.ShapeDtypeStruct((C, count * WIDE), F32),
        ],
        scratch_shapes=[pltpu.VMEM((comps, 32), BF16), pltpu.VMEM((C, comps), BF16)],
        compiler_params=pltpu.CompilerParams(vmem_limit_bytes=20 * MIB),
        name="tables",
    )(sky, fluxes, clusters, uvw, *after)


def model_kernel(me_ref, *rest):
    pieces, (pair_ref, pred_ref, gain_ref, model_ref, curv_ref, table) = rest[:4], rest[4:]
    owned = pieces[0].shape[0] // 8

    @pl.when(pl.program_id(0) == 0)
    def _():
        for n, piece in enumerate(pieces):
            flat = jnp.transpose(piece[...])
            high = flat.astype(BF16)
            at = pl.ds(n * flat.shape[1], flat.shape[1])
            table[pl.ds(0, flat.shape[0]), at] = high
            table[pl.ds(flat.shape[0], flat.shape[0]), at] = (
                flat - high.astype(F32)
            ).astype(BF16)
        curv_ref[...] = jnp.zeros_like(curv_ref)

    me = me_ref[0]
    my_y, my_z, my_core = me >> 3, (me >> 1) & 3, me & 1
    stations = table.shape[1]
    columns = table.shape[0] // 2
    ids = lax.broadcasted_iota(jnp.int32, (stations, BLOCK), 0)

    def gather(station):
        owner, own = station // owned, station % owned
        y, z, core = owner >> 3, (owner >> 1) & 3, owner & 1
        slot = ((((my_z - z) & 3) * 4 + ((my_y - y) & 3)) * 2 + (core ^ my_core)) * owned + own
        hot = jnp.where(ids == slot, 1.0, 0.0).astype(BF16)
        both = jnp.dot(table[...], hot, preferred_element_type=F32)
        return both[:columns] + both[columns:]

    first = gather(pair_ref[0:1, :])
    second = gather(pair_ref[1:2, :])
    rows = []
    curv = jnp.zeros((C, BLOCK), F32)
    for f in range(F):
        re, im = pl.ds(f * BLOCK, BLOCK), pl.ds((F + f) * BLOCK, BLOCK)
        p_re, p_im = first[f * C : (f + 1) * C], first[(F + f) * C : (F + f + 1) * C]
        q_re, q_im = second[f * C : (f + 1) * C], second[(F + f) * C : (F + f + 1) * C]
        g_re = p_re * q_re + p_im * q_im
        g_im = p_im * q_re - p_re * q_im
        gain_ref[:, re] = g_re
        gain_ref[:, im] = g_im
        cos_sum, sin_sum = pred_ref[:, re], pred_ref[:, im]
        rows.append(
            (
                jnp.sum(g_re * cos_sum + g_im * sin_sum, axis=0, keepdims=True),
                jnp.sum(g_im * cos_sum - g_re * sin_sum, axis=0, keepdims=True),
            )
        )
        curv = curv + (g_re * g_re + g_im * g_im)
    model = jnp.concatenate([r[0] for r in rows] + [r[1] for r in rows], axis=0)
    for n in range(model_ref.shape[0]):
        model_ref[n] = model
    curv_ref[...] += curv[:, :128] + curv[:, 128:]


def make_model(first, count, me, pieces, stations, pred, peers):
    whole = lambda i: (0, 0)
    rows, columns = pieces[0].shape
    return pl.pallas_call(
        model_kernel,
        grid=(count,),
        in_specs=[pl.BlockSpec(memory_space=pltpu.SMEM)]
        + [pl.BlockSpec((rows, columns), whole)] * 4
        + [
            pl.BlockSpec((2, BLOCK), lambda i: (0, i + first)),
            pl.BlockSpec((C, WIDE), lambda i: (0, i)),
        ],
        out_specs=[
            pl.BlockSpec((C, WIDE), lambda i: (0, i)),
            pl.BlockSpec((peers, 2 * F, BLOCK), lambda i: (0, 0, i)),
            pl.BlockSpec((C, 128), whole),
        ],
        out_shape=[
            jax.ShapeDtypeStruct((C, count * WIDE), F32),
            jax.ShapeDtypeStruct((peers, 2 * F, count * BLOCK), F32),
            jax.ShapeDtypeStruct((C, 128), F32),
        ],
        scratch_shapes=[pltpu.VMEM((2 * columns, 4 * rows), BF16)],
        compiler_params=pltpu.CompilerParams(vmem_limit_bytes=20 * MIB),
        name="model",
    )(me, *pieces, stations, pred)


def score_kernel(parts_ref, obs_ref, gain_ref, table_ref, clus_ref, *rest):
    *before, out_ref, total, weight = rest
    step = pl.program_id(0)
    curvs, earlier = before[: len(GROUPS)], before[len(GROUPS) :]

    @pl.when(step == 0)
    def _():
        total[...] = earlier[0][...] if earlier else jnp.zeros_like(total)

    model = jnp.sum(parts_ref[...], axis=0)
    for f in range(F):
        re, im = pl.ds(f * BLOCK, BLOCK), pl.ds((F + f) * BLOCK, BLOCK)
        r_re = obs_ref[0, f : f + 1, :] - model[f : f + 1, :]
        r_im = obs_ref[1, f : f + 1, :] - model[F + f : F + f + 1, :]
        g_re, g_im = gain_ref[:, re], gain_ref[:, im]
        weight[:, re] = (r_re * g_re + r_im * g_im).astype(BF16)
        weight[:, im] = (r_re * g_im - r_im * g_re).astype(BF16)
    total[...] += lax.dot_general(
        table_ref[...], weight[...], (((1,), (1,)), ((), ())), preferred_element_type=F32
    )

    @pl.when(step == pl.num_programs(0) - 1)
    def _():
        if not curvs:
            out_ref[...] = total[...]
            return
        scores = jnp.transpose(total[...])
        hot = lax.broadcasted_iota(jnp.int32, scores.shape, 0) == clus_ref[...]
        curv = jnp.sum(sum(c[...] for c in curvs), axis=1, keepdims=True)
        out_ref[0:1, :] = jnp.sum(jnp.where(hot, scores, 0.0), axis=0, keepdims=True)
        out_ref[1:2, :] = jnp.sum(jnp.where(hot, curv, 0.0), axis=0, keepdims=True)


def make_scores(first, count, parts, observed, gain, table, clusters, curvs, earlier):
    whole = lambda i: (0, 0)
    comps = table.shape[0]
    peers = parts.shape[0]
    shape = (2, comps) if curvs else (comps, C)
    return pl.pallas_call(
        score_kernel,
        grid=(count,),
        in_specs=[
            pl.BlockSpec((peers, 2 * F, BLOCK), lambda i: (0, 0, i)),
            pl.BlockSpec((2, F, BLOCK), lambda i: (0, 0, i + first)),
            pl.BlockSpec((C, WIDE), lambda i: (0, i)),
            pl.BlockSpec((comps, WIDE), lambda i: (0, i)),
            pl.BlockSpec((1, comps), whole),
        ]
        + [pl.BlockSpec((C, 128), whole)] * len(curvs)
        + [pl.BlockSpec((comps, C), whole)] * len(earlier),
        out_specs=pl.BlockSpec(shape, whole),
        out_shape=jax.ShapeDtypeStruct(shape, F32),
        scratch_shapes=[pltpu.VMEM((comps, C), F32), pltpu.VMEM((C, WIDE), BF16)],
        compiler_params=pltpu.CompilerParams(vmem_limit_bytes=20 * MIB),
        name="scores",
    )(parts, observed, gain, table, clusters, *curvs, *earlier)


def other_core():
    return [(i, i ^ 1) for i in range(32)]


def turn_y(k):
    return [(i, (i + 8 * k) % 32) for i in range(32)]


def turn_z(k):
    return [(i, i // 8 * 8 + ((i // 2 % 4 + k) % 4) * 2 + i % 2) for i in range(32)]


def plane_groups():
    return [[2 * i + core for i in range(16)] for core in range(2)]


def permute(x, pairs):
    return lax.ppermute(x, "row", pairs)


def per_device(
    baseline_uvw, sky_positions, fluxes, clusters, stations, station_gains, gain_step, observed_vis
):
    flux_row, cluster_row = fluxes[None, :], clusters[None, :]
    peers = lax.axis_size("comp")
    me = lax.axis_index("row").astype(jnp.int32)[None]
    firsts = [sum(GROUPS[:n]) for n in range(len(GROUPS))]

    owned = station_gains + gain_step
    chip = jnp.concatenate([owned, permute(owned, other_core())], axis=0)
    line = jnp.concatenate([chip] + [permute(chip, turn_y(k)) for k in (1, 2, 3)], axis=0)
    pieces = [line] + [permute(line, turn_z(k)) for k in (1, 2, 3)]

    after = ([chip], [line])
    tables, preds = zip(
        *(
            make_tables(
                firsts[n], GROUPS[n], sky_positions, flux_row, cluster_row, baseline_uvw, after[n]
            )
            for n in range(len(GROUPS))
        )
    )
    gains, models, curvs = zip(
        *(
            make_model(firsts[n], GROUPS[n], me, pieces, stations, preds[n], peers)
            for n in range(len(GROUPS))
        )
    )
    sent = [lax.all_to_all(m, "comp", 0, 0, tiled=True) for m in models]
    scores = ()
    for n in range(len(GROUPS)):
        last = n == len(GROUPS) - 1
        scores = (
            make_scores(
                firsts[n],
                GROUPS[n],
                sent[n],
                observed_vis,
                gains[n],
                tables[n],
                cluster_row,
                curvs if last else (),
                scores,
            ),
        )
    sums = scores[0]
    sums = sums + permute(sums, other_core())
    sums = lax.all_to_all(
        jnp.broadcast_to(sums[None], (16,) + sums.shape),
        "row",
        0,
        0,
        axis_index_groups=plane_groups(),
        tiled=True,
    ).sum(0)
    return fluxes + sums[0] / sums[1]


def solution(mesh):
    return jax.shard_map(
        per_device,
        mesh=mesh,
        in_specs=(
            P(None, "row"),
            P(None, "comp"),
            P("comp"),
            P("comp"),
            P(None, "row"),
            P("row", None),
            P("row", None),
            P(None, None, "row"),
        ),
        out_specs=P("comp"),
        check_vma=False,
    )
```

```python
import functools
import math

import jax
import jax.numpy as jnp
import numpy as np
from jax import lax
from jax.experimental import pallas as pl
from jax.experimental.pallas import tpu as pltpu
from jax.sharding import PartitionSpec as P

C = 64
F = 4
BLOCK = 256
WIDE = 2 * F * BLOCK
CHUNK = 256
TILE = 16
GROUPS = (4, 4)
SCOPED = 10 << 20
F32 = jnp.float32
BF16 = jnp.bfloat16


def sine_fit():
    y = 0.5 * np.cos(np.pi * (np.arange(400) + 0.5) / 400)
    fit = np.polynomial.polynomial.polyfit(y * y, 2.0 * np.sin(0.5 * np.pi * y) / y, 2)
    return [float(np.float32(v)) for v in fit]


ODD = sine_fit()
SCALES = (0.5, 0.25, 0.25, 0.25)
ROUND = 12582912.0


def split3(x):
    high = x.astype(BF16).astype(F32)
    rest = x - high
    mid = rest.astype(BF16).astype(F32)
    return high, mid, rest - mid


def left_terms(x):
    h, m, l = split3(x)
    return [h, h, m, h, l, m, m, l]


def right_terms(x):
    h, m, l = split3(x)
    return [h, m, h, l, h, m, l, m]


def stack_terms(terms):
    pad = jnp.zeros((8, terms[0].shape[1]), F32)
    return jnp.concatenate(terms + [pad], axis=0)


def phases(eighth):
    y = eighth - (jnp.round(eighth))
    y2 = y * y
    s = y * (ODD[0] + y2 * (ODD[1] + y2 * ODD[2]))
    cc = 4.0 - s * s
    s = s * (cc * lax.rsqrt(cc))
    c = cc - 2.0

    def double(c, s):
        return c * c - 2.0, s * c

    c1, s1 = double(c, s)
    c, s = double(c1, s1)
    c, s = double(c, s)
    c8, s8 = double(c, s)
    c9, s9 = c8 * c1 - s8 * s1, s8 * c1 + c8 * s1
    c10, s10 = c1 * c9 - (c8 + c8), c1 * s9 - (s8 + s8)
    c11, s11 = c1 * c10 - c9, c1 * s10 - s9
    return (c8, c9, c10, c11, s8, s9, s10, s11)


def table_kernel(first, count, sky_ref, flux_ref, clus_ref, uvw_ref, *rest):
    *table_refs, pred_ref, left, hot, late = rest[-(sky_ref.shape[1] // CHUNK + 4) :]
    comps = sky_ref.shape[1]
    chunks, tiles, pieces = comps // CHUNK, CHUNK // TILE, WIDE // CHUNK

    east, north = sky_ref[0:1, :], sky_ref[1:2, :]
    depth = jnp.sqrt(1.0 - east * east - north * north) - 1.0
    place = jnp.concatenate([east, north, depth], axis=0)
    left[...] = jnp.transpose(stack_terms(left_terms(place))).astype(BF16)
    ids = lax.broadcasted_iota(jnp.int32, (C, comps), 0)
    hot[...] = jnp.where(ids == clus_ref[...], flux_ref[...], 0.0).astype(BF16)
    late[...] = jnp.zeros_like(late)
    last = chunks - 1

    def matmul(i, chunk, n):
        at, to = pl.ds(chunk * CHUNK, CHUNK), pl.ds(n * CHUNK, CHUNK)
        source = late[:, to] if chunk == last else table_refs[chunk][i, :, to]
        part = jnp.dot(hot[:, at], source, preferred_element_type=F32)
        if chunk == 0:
            pred_ref[i, :, to] = part
        else:
            pred_ref[i, :, to] += part

    def block(i, carry):
        before = jnp.maximum(i - 1, 0)
        uvw = uvw_ref[:, pl.ds(pl.multiple_of((i + first) * BLOCK, BLOCK), BLOCK)]
        right = stack_terms(right_terms(uvw * 0.125)).astype(BF16)
        for chunk in range(chunks):
            base = jnp.dot(
                left[pl.ds(chunk * CHUNK, CHUNK), :], right, preferred_element_type=F32
            )
            for tile in range(tiles):
                values = phases(base[tile * TILE : (tile + 1) * TILE, :])
                for j, value in enumerate(values):
                    value = value.astype(BF16)
                    to = pl.ds(j * BLOCK, BLOCK)
                    table_refs[chunk][i, pl.ds(tile * TILE, TILE), to] = value
                    if chunk == last:
                        late[pl.ds(tile * TILE, TILE), to] = value
                if tile % (tiles // pieces) == 0:
                    n = tile // (tiles // pieces)
                    if chunk:
                        matmul(i, chunk - 1, n)
                    else:
                        matmul(before, last, n)
        return carry

    pred_ref[0] = jnp.zeros(pred_ref.shape[1:], F32)
    lax.fori_loop(0, count, block, 0)
    for n in range(pieces):
        matmul(count - 1, last, n)


def in_vmem(x):
    return pltpu.with_memory_space_constraint(x, pltpu.VMEM)


def make_tables(first, count, sky, fluxes, clusters, uvw, after, held):
    comps = sky.shape[1]
    vmem = pl.BlockSpec(memory_space=pltpu.VMEM)
    chunks = comps // CHUNK
    return pl.pallas_call(
        functools.partial(table_kernel, first, count),
        in_specs=[vmem] * (4 + len(held)) + [pl.BlockSpec(memory_space=pl.ANY)] * len(after),
        out_specs=[vmem] * (chunks + 1),
        out_shape=[pltpu.VMEM((count, CHUNK, WIDE), BF16)] * chunks
        + [pltpu.VMEM((count, C, WIDE), F32)],
        scratch_shapes=[
            pltpu.VMEM((comps, 32), BF16),
            pltpu.VMEM((C, comps), BF16),
            pltpu.VMEM((CHUNK, WIDE), BF16),
        ],
        compiler_params=pltpu.CompilerParams(vmem_limit_bytes=SCOPED),
        name="tables",
    )(sky, fluxes, clusters, uvw, *map(in_vmem, held), *after)


def model_kernel(me_ref, *rest):
    pieces, pair_ref, preds = rest[:4], rest[4], rest[5 : 5 + len(GROUPS)]
    gain_ref, model_ref, curv_ref, table, found = rest[-5:]
    owned = pieces[0].shape[0] // 8
    for n, piece in enumerate(pieces):
        flat = jnp.transpose(piece[...])
        high = flat.astype(BF16)
        at = pl.ds(n * flat.shape[1], flat.shape[1])
        table[pl.ds(0, flat.shape[0]), at] = high
        table[pl.ds(flat.shape[0], flat.shape[0]), at] = (flat - high.astype(F32)).astype(BF16)

    me = me_ref[0]
    my_y, my_z, my_core = me >> 3, (me >> 1) & 3, me & 1
    stations = table.shape[1]
    columns = table.shape[0] // 2
    ids = lax.broadcasted_iota(jnp.int32, (stations, BLOCK), 0)
    pair = pair_ref[...]
    owner, own = pair // owned, pair % owned
    y, z, core = owner >> 3, (owner >> 1) & 3, owner & 1
    slot = ((((my_z - z) & 3) * 4 + ((my_y - y) & 3)) * 2 + (core ^ my_core)) * owned + own

    def gather(i):
        for side in range(2):
            hot = ids == slot[side : side + 1, i * BLOCK : (i + 1) * BLOCK]
            hot = jnp.where(hot, 1.0, 0.0).astype(BF16)
            both = jnp.dot(table[...], hot, preferred_element_type=F32)
            found[i % 2, side] = both[:columns] + both[columns:]

    curv = jnp.zeros((C, BLOCK), F32)
    count = gain_ref.shape[0]
    gather(0)
    blocks = [(pred, i) for pred in preds for i in range(pred.shape[0])]
    for i, (pred_ref, own_i) in enumerate(blocks):
        if i + 1 < count:
            gather(i + 1)
        rows = []
        for f in range(F):
            re, im = pl.ds(f * BLOCK, BLOCK), pl.ds((F + f) * BLOCK, BLOCK)
            at_re, at_im = pl.ds(f * C, C), pl.ds((F + f) * C, C)
            p_re, p_im = found[i % 2, 0, at_re], found[i % 2, 0, at_im]
            q_re, q_im = found[i % 2, 1, at_re], found[i % 2, 1, at_im]
            g_re = p_re * q_re + p_im * q_im
            g_im = p_im * q_re - p_re * q_im
            gain_ref[i, :, re] = g_re
            gain_ref[i, :, im] = g_im
            cos_sum, sin_sum = pred_ref[own_i, :, re], pred_ref[own_i, :, im]
            rows.append(
                (
                    SCALES[f] * jnp.sum(g_re * cos_sum + g_im * sin_sum, axis=0, keepdims=True),
                    SCALES[f] * jnp.sum(g_im * cos_sum - g_re * sin_sum, axis=0, keepdims=True),
                )
            )
            curv = curv + (g_re * g_re + g_im * g_im)
        model = jnp.concatenate([r[0] for r in rows] + [r[1] for r in rows], axis=0)
        for n in range(model_ref.shape[0]):
            model_ref[n, :, pl.ds(i * BLOCK, BLOCK)] = model
    curv_ref[...] = curv[:, :128] + curv[:, 128:]


def make_model(me, pieces, stations, preds, held, peers):
    rows, columns = pieces[0].shape
    count = sum(pred.shape[0] for pred in preds)
    vmem = pl.BlockSpec(memory_space=pltpu.VMEM)
    return pl.pallas_call(
        model_kernel,
        in_specs=[pl.BlockSpec(memory_space=pltpu.SMEM)] + [vmem] * (5 + len(preds) + len(held)),
        out_specs=[vmem] * 3,
        out_shape=[
            pltpu.VMEM((count, C, WIDE), F32),
            jax.ShapeDtypeStruct((peers, 2 * F, count * BLOCK), F32),
            jax.ShapeDtypeStruct((C, 128), F32),
        ],
        scratch_shapes=[
            pltpu.VMEM((2 * columns, 4 * rows), BF16),
            pltpu.VMEM((2, 2, columns, BLOCK), F32),
        ],
        compiler_params=pltpu.CompilerParams(vmem_limit_bytes=SCOPED),
        name="model",
    )(me, *pieces, stations, *map(in_vmem, preds), *map(in_vmem, held))


def score_kernel(parts_ref, obs_ref, gain_ref, clus_ref, curv_ref, *rest):
    *tables, out_ref, weight = rest
    chunks = len(tables) // len(GROUPS)
    blocks = [
        (tables[n * chunks : (n + 1) * chunks], i) for n in range(len(GROUPS)) for i in range(GROUPS[n])
    ]

    def weigh(i):
        at = pl.ds(i * BLOCK, BLOCK)
        model = jnp.sum(parts_ref[:, :, at], axis=0)
        for f in range(F):
            re, im = pl.ds(f * BLOCK, BLOCK), pl.ds((F + f) * BLOCK, BLOCK)
            r_re = SCALES[f] * (obs_ref[0, f : f + 1, at] - model[f : f + 1, :])
            r_im = SCALES[f] * (obs_ref[1, f : f + 1, at] - model[F + f : F + f + 1, :])
            g_re, g_im = gain_ref[i, :, re], gain_ref[i, :, im]
            weight[i % 2, :, re] = (r_re * g_re + r_im * g_im).astype(BF16)
            weight[i % 2, :, im] = (r_re * g_im - r_im * g_re).astype(BF16)

    weigh(0)
    scores = [jnp.zeros((C, CHUNK), F32)] * chunks
    for i, (group, own_i) in enumerate(blocks):
        for n in range(chunks):
            scores[n] = scores[n] + lax.dot_general(
                weight[i % 2], group[n][own_i], (((1,), (1,)), ((), ())), preferred_element_type=F32
            )
        if i + 1 < len(blocks):
            weigh(i + 1)
    scores = jnp.concatenate(scores, axis=1)
    hot = lax.broadcasted_iota(jnp.int32, scores.shape, 0) == clus_ref[...]
    curv = jnp.sum(curv_ref[...], axis=1, keepdims=True)
    out_ref[0:1, :] = jnp.sum(jnp.where(hot, scores, 0.0), axis=0, keepdims=True)
    out_ref[1:2, :] = jnp.sum(jnp.where(hot, curv, 0.0), axis=0, keepdims=True)


def make_scores(parts, observed, gain, clusters, curv, tables):
    comps = clusters.shape[1]
    vmem = pl.BlockSpec(memory_space=pltpu.VMEM)
    return pl.pallas_call(
        score_kernel,
        in_specs=[vmem] * (5 + len(tables)),
        out_specs=vmem,
        out_shape=jax.ShapeDtypeStruct((2, comps), F32),
        scratch_shapes=[pltpu.VMEM((2, C, WIDE), BF16)],
        compiler_params=pltpu.CompilerParams(vmem_limit_bytes=SCOPED),
        name="scores",
    )(parts, observed, in_vmem(gain), clusters, curv, *map(in_vmem, tables))


def other_core():
    return [(i, i ^ 1) for i in range(32)]


def turn_y(k):
    return [(i, (i + 8 * k) % 32) for i in range(32)]


def turn_z(k):
    return [(i, i // 8 * 8 + ((i // 2 % 4 + k) % 4) * 2 + i % 2) for i in range(32)]


def plane_groups():
    return [[2 * i + core for i in range(16)] for core in range(2)]


def permute(x, pairs):
    return lax.ppermute(x, "row", pairs)


def per_device(
    baseline_uvw, sky_positions, fluxes, clusters, stations, station_gains, gain_step, observed_vis
):
    flux_row, cluster_row = fluxes[None, :], clusters[None, :]
    peers = lax.axis_size("comp")
    me = lax.axis_index("row").astype(jnp.int32)[None]
    firsts = [sum(GROUPS[:n]) for n in range(len(GROUPS))]

    owned = station_gains + gain_step
    chip = jnp.concatenate([owned, permute(owned, other_core())], axis=0)
    line = jnp.concatenate([chip] + [permute(chip, turn_y(k)) for k in (1, 2, 3)], axis=0)
    pieces = [line] + [permute(line, turn_z(k)) for k in (1, 2, 3)]

    after = ([chip], [line])
    tables, preds = [], []
    for n, count in enumerate(GROUPS):
        *parts, pred = make_tables(
            firsts[n],
            count,
            sky_positions,
            flux_row,
            cluster_row,
            baseline_uvw,
            after[n],
            tables + preds,
        )
        tables += parts
        preds.append(pred)
    gain, model, curv = make_model(me, pieces, stations, preds, tables, peers)
    parts = lax.all_to_all(model, "comp", 0, 0, tiled=True)
    sums = make_scores(parts, observed_vis, gain, cluster_row, curv, tables)
    sums = sums + permute(sums, other_core())
    sums = lax.all_to_all(
        jnp.broadcast_to(sums[None], (16,) + sums.shape),
        "row",
        0,
        0,
        axis_index_groups=plane_groups(),
        tiled=True,
    ).sum(0)
    return fluxes + sums[0] / sums[1]


def solution(mesh):
    return jax.shard_map(
        per_device,
        mesh=mesh,
        in_specs=(
            P(None, "row"),
            P(None, "comp"),
            P("comp"),
            P("comp"),
            P(None, "row"),
            P("row", None),
            P("row", None),
            P(None, None, "row"),
        ),
        out_specs=P("comp"),
        check_vma=False,
    )
```

```python
import functools
import math

import jax
import jax.numpy as jnp
import numpy as np
from jax import lax
from jax.experimental import pallas as pl
from jax.experimental.pallas import tpu as pltpu
from jax.sharding import PartitionSpec as P

C = 64
F = 4
BLOCK = 256
WIDE = 2 * F * BLOCK
CHUNK = 256
TILE = 16
GROUPS = (4, 4)
SCOPED = 10 << 20
F32 = jnp.float32
BF16 = jnp.bfloat16


def sine_fit():
    y = 0.5 * np.cos(np.pi * (np.arange(400) + 0.5) / 400)
    fit = np.polynomial.polynomial.polyfit(y * y, 2.0 * np.sin(0.5 * np.pi * y) / y, 2)
    return [float(np.float32(v)) for v in fit]


ODD = sine_fit()
SCALES = (0.5, 0.25, 0.25, 0.25)
ROUND = 12582912.0


def split3(x):
    high = x.astype(BF16).astype(F32)
    rest = x - high
    mid = rest.astype(BF16).astype(F32)
    return high, mid, rest - mid


def left_terms(x):
    h, m, l = split3(x)
    return [h, h, m, h, l, m, m, l]


def right_terms(x):
    h, m, l = split3(x)
    return [h, m, h, l, h, m, l, m]


def stack_terms(terms):
    pad = jnp.zeros((8, terms[0].shape[1]), F32)
    return jnp.concatenate(terms + [pad], axis=0)


def phases(eighth):
    y = eighth - (jnp.round(eighth))
    y2 = y * y
    s = y * (ODD[0] + y2 * (ODD[1] + y2 * ODD[2]))
    cc = 4.0 - s * s
    s = s * (cc * lax.rsqrt(cc))
    c = cc - 2.0

    def double(c, s):
        return c * c - 2.0, s * c

    c1, s1 = double(c, s)
    c, s = double(c1, s1)
    c, s = double(c, s)
    c8, s8 = double(c, s)
    c9, s9 = c8 * c1 - s8 * s1, s8 * c1 + c8 * s1
    c10, s10 = c1 * c9 - (c8 + c8), c1 * s9 - (s8 + s8)
    c11, s11 = c1 * c10 - c9, c1 * s10 - s9
    return (c8, c9, c10, c11, s8, s9, s10, s11)


def table_kernel(first, count, me_ref, sky_ref, flux_ref, clus_ref, uvw_ref, pass_ref, *rest):
    *table_refs, pred_ref, passed, place_ref, baseline, base, hot, late = rest[
        -(sky_ref.shape[1] // CHUNK + 7) :
    ]
    passed[...] = pass_ref[0 : passed.shape[0], :]
    comps = sky_ref.shape[1]
    chunks, tiles, pieces = comps // CHUNK, BLOCK // TILE, WIDE // BLOCK

    east, north = sky_ref[0:1, :], sky_ref[1:2, :]
    depth = jnp.sqrt(1.0 - east * east - north * north) - 1.0
    place = jnp.concatenate([east, north, depth], axis=0)
    place_ref[...] = stack_terms(left_terms(place)).astype(BF16)
    ids = lax.broadcasted_iota(jnp.int32, (C, comps), 0)
    hot[...] = jnp.where(ids == clus_ref[...], flux_ref[...], 0.0).astype(BF16)
    late[...] = jnp.zeros_like(late)
    last = chunks - 1
    dims = (((1,), (1,)), ((), ()))

    def matmul(i, chunk, n):
        at, to = pl.ds(chunk * CHUNK, CHUNK), pl.ds(n * BLOCK, BLOCK)
        source = late[to, :] if chunk == last else table_refs[chunk][i, to, :]
        part = lax.dot_general(hot[:, at], source, dims, preferred_element_type=F32)
        if chunk == 0:
            pred_ref[i, :, to] = part
        else:
            pred_ref[i, :, to] += part

    def turn(i):
        uvw = uvw_ref[:, pl.ds(pl.multiple_of((i + first) * BLOCK, BLOCK), BLOCK)]
        baseline[...] = jnp.transpose(stack_terms(right_terms(uvw * 0.125))).astype(BF16)

    def project(chunk):
        base[chunk % 2] = jnp.dot(
            baseline[...], place_ref[:, pl.ds(chunk * CHUNK, CHUNK)], preferred_element_type=F32
        )

    def block(i, carry):
        before = jnp.maximum(i - 1, 0)
        for chunk in range(chunks):
            if chunk == last:
                turn(jnp.minimum(i + 1, count - 1))
            project((chunk + 1) % chunks)
            for tile in range(tiles):
                values = phases(base[chunk % 2, pl.ds(tile * TILE, TILE), :])
                for j, value in enumerate(values):
                    value = value.astype(BF16)
                    to = pl.ds(j * BLOCK + tile * TILE, TILE)
                    table_refs[chunk][i, to, :] = value
                    if chunk == last:
                        late[to, :] = value
                if tile % (tiles // pieces) == 0:
                    n = tile // (tiles // pieces)
                    if chunk:
                        matmul(i, chunk - 1, n)
                    else:
                        matmul(before, last, n)
        return carry

    pred_ref[0] = jnp.zeros(pred_ref.shape[1:], F32)
    turn(0)
    project(0)
    lax.fori_loop(0, count, block, 0)
    for n in range(pieces):
        matmul(count - 1, last, n)


def in_vmem(x):
    return pltpu.with_memory_space_constraint(x, pltpu.VMEM)


def make_tables(first, count, me, sky, fluxes, clusters, uvw, after, passed, held):
    comps = sky.shape[1]
    vmem = pl.BlockSpec(memory_space=pltpu.VMEM)
    chunks = comps // CHUNK
    return pl.pallas_call(
        functools.partial(table_kernel, first, count),
        in_specs=[pl.BlockSpec(memory_space=pltpu.SMEM)] + [vmem] * (5 + len(held)),
        out_specs=[vmem] * (chunks + 2),
        out_shape=[pltpu.VMEM((count, WIDE, CHUNK), BF16)] * chunks
        + [
            pltpu.VMEM((count, C, WIDE), F32),
            jax.ShapeDtypeStruct((passed, after.shape[1]), F32),
        ],
        scratch_shapes=[
            pltpu.VMEM((32, comps), BF16),
            pltpu.VMEM((BLOCK, 32), BF16),
            pltpu.VMEM((2, BLOCK, CHUNK), F32),
            pltpu.VMEM((C, comps), BF16),
            pltpu.VMEM((WIDE, CHUNK), BF16),
        ],
        compiler_params=pltpu.CompilerParams(vmem_limit_bytes=SCOPED),
        cost_estimate=pl.CostEstimate(
            flops=2 * C * comps * count * WIDE,
            bytes_accessed=2 * comps * count * WIDE,
            transcendentals=4 * comps * count * WIDE,
        ),
        name="tables",
    )(me, sky, fluxes, clusters, uvw, after, *map(in_vmem, held))


def model_kernel(me_ref, *rest):
    pieces, pair_ref, preds = rest[:4], rest[4], rest[5 : 5 + len(GROUPS)]
    gain_ref, model_ref, curv_ref, table, found = rest[-5:]
    owned = pieces[0].shape[0] // 8
    for n, piece in enumerate(pieces):
        flat = jnp.transpose(piece[...])
        high = flat.astype(BF16)
        at = pl.ds(n * flat.shape[1], flat.shape[1])
        table[pl.ds(0, flat.shape[0]), at] = high
        table[pl.ds(flat.shape[0], flat.shape[0]), at] = (flat - high.astype(F32)).astype(BF16)

    me = me_ref[0]
    my_y, my_z, my_core = me >> 3, (me >> 1) & 3, me & 1
    stations = table.shape[1]
    columns = table.shape[0] // 2
    ids = lax.broadcasted_iota(jnp.int32, (stations, BLOCK), 0)
    pair = pair_ref[...]
    owner, own = pair // owned, pair % owned
    y, z, core = owner >> 3, (owner >> 1) & 3, owner & 1
    slot = ((((my_z - z) & 3) * 4 + ((my_y - y) & 3)) * 2 + (core ^ my_core)) * owned + own

    def gather(i):
        for side in range(2):
            hot = ids == slot[side : side + 1, i * BLOCK : (i + 1) * BLOCK]
            hot = jnp.where(hot, 1.0, 0.0).astype(BF16)
            both = jnp.dot(table[...], hot, preferred_element_type=F32)
            found[i % 2, side] = both[:columns] + both[columns:]

    curv = jnp.zeros((C, BLOCK), F32)
    count = gain_ref.shape[0]
    gather(0)
    blocks = [(pred, i) for pred in preds for i in range(pred.shape[0])]
    for i, (pred_ref, own_i) in enumerate(blocks):
        if i + 1 < count:
            gather(i + 1)
        rows = []
        for f in range(F):
            re, im = pl.ds(f * BLOCK, BLOCK), pl.ds((F + f) * BLOCK, BLOCK)
            at_re, at_im = pl.ds(f * C, C), pl.ds((F + f) * C, C)
            p_re, p_im = found[i % 2, 0, at_re], found[i % 2, 0, at_im]
            q_re, q_im = found[i % 2, 1, at_re], found[i % 2, 1, at_im]
            g_re = p_re * q_re + p_im * q_im
            g_im = p_im * q_re - p_re * q_im
            gain_ref[i, :, re] = g_re
            gain_ref[i, :, im] = g_im
            cos_sum, sin_sum = pred_ref[own_i, :, re], pred_ref[own_i, :, im]
            rows.append(
                (
                    SCALES[f] * jnp.sum(g_re * cos_sum + g_im * sin_sum, axis=0, keepdims=True),
                    SCALES[f] * jnp.sum(g_im * cos_sum - g_re * sin_sum, axis=0, keepdims=True),
                )
            )
            curv = curv + (g_re * g_re + g_im * g_im)
        model = jnp.concatenate([r[0] for r in rows] + [r[1] for r in rows], axis=0)
        for n in range(model_ref.shape[0]):
            model_ref[n, :, pl.ds(i * BLOCK, BLOCK)] = model
    curv_ref[...] = curv[:, :128] + curv[:, 128:]


def make_model(me, pieces, stations, preds, held, peers):
    rows, columns = pieces[0].shape
    count = sum(pred.shape[0] for pred in preds)
    vmem = pl.BlockSpec(memory_space=pltpu.VMEM)
    return pl.pallas_call(
        model_kernel,
        in_specs=[pl.BlockSpec(memory_space=pltpu.SMEM)] + [vmem] * (5 + len(preds) + len(held)),
        out_specs=[vmem] * 3,
        out_shape=[
            pltpu.VMEM((count, C, WIDE), F32),
            jax.ShapeDtypeStruct((peers, 2 * F, count * BLOCK), F32),
            jax.ShapeDtypeStruct((C, 128), F32),
        ],
        scratch_shapes=[
            pltpu.VMEM((2 * columns, 4 * rows), BF16),
            pltpu.VMEM((2, 2, columns, BLOCK), F32),
        ],
        compiler_params=pltpu.CompilerParams(vmem_limit_bytes=SCOPED),
        name="model",
    )(me, *pieces, stations, *map(in_vmem, preds), *map(in_vmem, held))


def score_kernel(parts_ref, obs_ref, gain_ref, clus_ref, curv_ref, *rest):
    *tables, out_ref, weight = rest
    chunks = len(tables) // len(GROUPS)
    blocks = [
        (tables[n * chunks : (n + 1) * chunks], i) for n in range(len(GROUPS)) for i in range(GROUPS[n])
    ]

    def weigh(i):
        at = pl.ds(i * BLOCK, BLOCK)
        model = jnp.sum(parts_ref[:, :, at], axis=0)
        for f in range(F):
            re, im = pl.ds(f * BLOCK, BLOCK), pl.ds((F + f) * BLOCK, BLOCK)
            r_re = SCALES[f] * (obs_ref[0, f : f + 1, at] - model[f : f + 1, :])
            r_im = SCALES[f] * (obs_ref[1, f : f + 1, at] - model[F + f : F + f + 1, :])
            g_re, g_im = gain_ref[i, :, re], gain_ref[i, :, im]
            weight[i % 2, :, re] = (r_re * g_re + r_im * g_im).astype(BF16)
            weight[i % 2, :, im] = (r_re * g_im - r_im * g_re).astype(BF16)

    weigh(0)
    scores = [jnp.zeros((C, CHUNK), F32)] * chunks
    for i, (group, own_i) in enumerate(blocks):
        for n in range(chunks):
            scores[n] = scores[n] + jnp.dot(
                weight[i % 2], group[n][own_i], preferred_element_type=F32
            )
        if i + 1 < len(blocks):
            weigh(i + 1)
    scores = jnp.concatenate(scores, axis=1)
    hot = lax.broadcasted_iota(jnp.int32, scores.shape, 0) == clus_ref[...]
    curv = jnp.sum(curv_ref[...], axis=1, keepdims=True)
    out_ref[0:1, :] = jnp.sum(jnp.where(hot, scores, 0.0), axis=0, keepdims=True)
    out_ref[1:2, :] = jnp.sum(jnp.where(hot, curv, 0.0), axis=0, keepdims=True)


def make_scores(parts, observed, gain, clusters, curv, tables):
    comps = clusters.shape[1]
    vmem = pl.BlockSpec(memory_space=pltpu.VMEM)
    return pl.pallas_call(
        score_kernel,
        in_specs=[vmem] * (5 + len(tables)),
        out_specs=vmem,
        out_shape=jax.ShapeDtypeStruct((2, comps), F32),
        scratch_shapes=[pltpu.VMEM((2, C, WIDE), BF16)],
        compiler_params=pltpu.CompilerParams(vmem_limit_bytes=SCOPED),
        name="scores",
    )(parts, observed, in_vmem(gain), clusters, curv, *map(in_vmem, tables))


def other_core():
    return [(i, i ^ 1) for i in range(32)]


def turn_y(k):
    return [(i, (i + 8 * k) % 32) for i in range(32)]


def turn_z(k):
    return [(i, i // 8 * 8 + ((i // 2 % 4 + k) % 4) * 2 + i % 2) for i in range(32)]


def plane_groups():
    return [[2 * i + core for i in range(16)] for core in range(2)]


def permute(x, pairs):
    return lax.ppermute(x, "row", pairs)


def per_device(
    baseline_uvw, sky_positions, fluxes, clusters, stations, station_gains, gain_step, observed_vis
):
    flux_row, cluster_row = fluxes[None, :], clusters[None, :]
    peers = lax.axis_size("comp")
    me = lax.axis_index("row").astype(jnp.int32)[None]
    firsts = [sum(GROUPS[:n]) for n in range(len(GROUPS))]

    owned = station_gains + gain_step
    chip = jnp.concatenate([owned, permute(owned, other_core())], axis=0)
    others = [permute(chip, turn_y(k)) for k in (1, 2, 3)]
    tables, preds = [], []
    after, passed = chip, chip.shape[0]
    for n, count in enumerate(GROUPS):
        *parts, pred, after = make_tables(
            firsts[n],
            count,
            me,
            sky_positions,
            flux_row,
            cluster_row,
            baseline_uvw,
            after,
            passed,
            tables + preds,
        )
        tables += parts
        preds.append(pred)
        if n == 0:
            after = jnp.concatenate([after] + others, axis=0)
            pieces = [after] + [permute(after, turn_z(k)) for k in (1, 2, 3)]
            passed = 8
    gain, model, curv = make_model(me, pieces, stations, preds, tables, peers)
    parts = lax.all_to_all(model, "comp", 0, 0, tiled=True)
    sums = make_scores(parts, observed_vis, gain, cluster_row, curv, tables)
    sums = sums + permute(sums, other_core())
    sums = lax.all_to_all(
        jnp.broadcast_to(sums[None], (16,) + sums.shape),
        "row",
        0,
        0,
        axis_index_groups=plane_groups(),
        tiled=True,
    ).sum(0)
    return fluxes + sums[0] / sums[1]


def solution(mesh):
    return jax.shard_map(
        per_device,
        mesh=mesh,
        in_specs=(
            P(None, "row"),
            P(None, "comp"),
            P("comp"),
            P("comp"),
            P(None, "row"),
            P("row", None),
            P("row", None),
            P(None, None, "row"),
        ),
        out_specs=P("comp"),
        check_vma=False,
    )
```

```python
import functools
import math

import jax
import jax.numpy as jnp
import numpy as np
from jax import lax
from jax.experimental import pallas as pl
from jax.experimental.pallas import tpu as pltpu
from jax.sharding import PartitionSpec as P

C = 64
F = 4
BLOCK = 256
WIDE = 2 * F * BLOCK
CHUNK = 256
TILE = 16
GROUPS = (4, 4)
SCOPED = 10 << 20
F32 = jnp.float32
BF16 = jnp.bfloat16


def sine_fit():
    y = 0.5 * np.cos(np.pi * (np.arange(400) + 0.5) / 400)
    fit = np.polynomial.polynomial.polyfit(y * y, 2.0 * np.sin(0.5 * np.pi * y) / y, 2)
    return [float(np.float32(v)) for v in fit]


ODD = sine_fit()
SCALES = (0.5, 0.25, 0.25, 0.25)
ROUND = 12582912.0


def split3(x):
    high = x.astype(BF16).astype(F32)
    rest = x - high
    mid = rest.astype(BF16).astype(F32)
    return high, mid, rest - mid


def left_terms(x):
    h, m, l = split3(x)
    return [h, h, m, h, l, m, m, l]


def right_terms(x):
    h, m, l = split3(x)
    return [h, m, h, l, h, m, l, m]


def stack_terms(terms):
    pad = jnp.zeros((8, terms[0].shape[1]), F32)
    return jnp.concatenate(terms + [pad], axis=0)


def phases(eighth):
    y = eighth - (jnp.round(eighth))
    y2 = y * y
    s = y * (ODD[0] + y2 * (ODD[1] + y2 * ODD[2]))
    cc = 4.0 - s * s
    s = s * (cc * lax.rsqrt(cc))
    c = cc - 2.0

    def double(c, s):
        return c * c - 2.0, s * c

    c1, s1 = double(c, s)
    c, s = double(c1, s1)
    c, s = double(c, s)
    c8, s8 = double(c, s)
    c9, s9 = c8 * c1 - s8 * s1, s8 * c1 + c8 * s1
    c10, s10 = c1 * c9 - (c8 + c8), c1 * s9 - (s8 + s8)
    c11, s11 = c1 * c10 - c9, c1 * s10 - s9
    return (c8, c9, c10, c11, s8, s9, s10, s11)


def table_kernel(first, count, me_ref, sky_ref, flux_ref, clus_ref, uvw_ref, pass_ref, *rest):
    *table_refs, pred_ref, passed, place_ref, hot = rest[-(sky_ref.shape[1] // CHUNK + 4) :]
    passed[...] = pass_ref[...]
    comps = sky_ref.shape[1]
    chunks, tiles, pieces = comps // CHUNK, BLOCK // TILE, WIDE // BLOCK

    east, north = sky_ref[0:1, :], sky_ref[1:2, :]
    depth = jnp.sqrt(1.0 - east * east - north * north) - 1.0
    place = jnp.concatenate([east, north, depth], axis=0)
    place_ref[...] = stack_terms(left_terms(place)).astype(BF16)
    ids = lax.broadcasted_iota(jnp.int32, (C, comps), 0)
    hot[...] = jnp.where(ids == clus_ref[...], flux_ref[...], 0.0).astype(BF16)
    dims = (((1,), (1,)), ((), ()))

    def matmul(i, n):
        to = pl.ds(n * BLOCK, BLOCK)
        part = jnp.zeros((C, BLOCK), F32)
        for chunk in range(chunks):
            part = part + lax.dot_general(
                hot[:, pl.ds(chunk * CHUNK, CHUNK)],
                table_refs[chunk][i, to, :],
                dims,
                preferred_element_type=F32,
            )
        pred_ref[i, :, to] = part

    for i in range(count):
        uvw = uvw_ref[:, pl.ds((i + first) * BLOCK, BLOCK)]
        baseline = jnp.transpose(stack_terms(right_terms(uvw * 0.125))).astype(BF16)
        for chunk in range(chunks):
            base = jnp.dot(
                baseline, place_ref[:, pl.ds(chunk * CHUNK, CHUNK)], preferred_element_type=F32
            )
            for tile in range(tiles):
                values = phases(base[tile * TILE : (tile + 1) * TILE, :])
                for j, value in enumerate(values):
                    to = pl.ds(j * BLOCK + tile * TILE, TILE)
                    table_refs[chunk][i, to, :] = value.astype(BF16)
                done = chunk * tiles + tile
                each = chunks * tiles // pieces
                if i and done % each == each - 1:
                    matmul(i - 1, done // each)
    for n in range(pieces):
        matmul(count - 1, n)


def in_vmem(x):
    return pltpu.with_memory_space_constraint(x, pltpu.VMEM)


def make_tables(first, count, me, sky, fluxes, clusters, uvw, after, held):
    comps = sky.shape[1]
    vmem = pl.BlockSpec(memory_space=pltpu.VMEM)
    chunks = comps // CHUNK
    return pl.pallas_call(
        functools.partial(table_kernel, first, count),
        in_specs=[pl.BlockSpec(memory_space=pltpu.SMEM)] + [vmem] * (5 + len(held)),
        out_specs=[vmem] * (chunks + 2),
        out_shape=[pltpu.VMEM((count, WIDE, CHUNK), BF16)] * chunks
        + [
            pltpu.VMEM((count, C, WIDE), F32),
            jax.ShapeDtypeStruct(after.shape, F32),
        ],
        scratch_shapes=[
            pltpu.VMEM((32, comps), BF16),
            pltpu.VMEM((C, comps), BF16),
        ],
        compiler_params=pltpu.CompilerParams(vmem_limit_bytes=SCOPED),
        cost_estimate=pl.CostEstimate(
            flops=2 * C * comps * count * WIDE,
            bytes_accessed=2 * comps * count * WIDE,
            transcendentals=4 * comps * count * WIDE,
        ),
        name="tables",
    )(me, sky, fluxes, clusters, uvw, after, *map(in_vmem, held))


def model_kernel(me_ref, *rest):
    pieces, pair_ref, preds = rest[:2], rest[2], rest[3 : 3 + len(GROUPS)]
    gain_ref, model_ref, curv_ref, table, found = rest[-5:]
    owned = pieces[0].shape[0] // 16
    for n, piece in enumerate(pieces):
        flat = jnp.transpose(piece[...])
        high = flat.astype(BF16)
        at = pl.ds(n * flat.shape[1], flat.shape[1])
        table[pl.ds(0, flat.shape[0]), at] = high
        table[pl.ds(flat.shape[0], flat.shape[0]), at] = (flat - high.astype(F32)).astype(BF16)

    me = me_ref[0]
    my_y, my_z, my_core = me >> 3, (me >> 1) & 3, me & 1
    stations = table.shape[1]
    columns = table.shape[0] // 2
    ids = lax.broadcasted_iota(jnp.int32, (stations, BLOCK), 0)
    pair = pair_ref[...]
    owner, own = pair // owned, pair % owned
    y, z, core = owner >> 3, (owner >> 1) & 3, owner & 1
    slot = (((core ^ my_core) * 4 + ((my_y - y) & 3)) * 4 + ((my_z - z) & 3)) * owned + own

    def gather(i):
        for side in range(2):
            hot = ids == slot[side : side + 1, i * BLOCK : (i + 1) * BLOCK]
            hot = jnp.where(hot, 1.0, 0.0).astype(BF16)
            both = jnp.dot(table[...], hot, preferred_element_type=F32)
            found[i % 2, side] = both[:columns] + both[columns:]

    curv = jnp.zeros((C, BLOCK), F32)
    count = gain_ref.shape[0]
    gather(0)
    blocks = [(pred, i) for pred in preds for i in range(pred.shape[0])]
    for i, (pred_ref, own_i) in enumerate(blocks):
        if i + 1 < count:
            gather(i + 1)
        rows = []
        for f in range(F):
            re, im = pl.ds(f * BLOCK, BLOCK), pl.ds((F + f) * BLOCK, BLOCK)
            at_re, at_im = pl.ds(f * C, C), pl.ds((F + f) * C, C)
            p_re, p_im = found[i % 2, 0, at_re], found[i % 2, 0, at_im]
            q_re, q_im = found[i % 2, 1, at_re], found[i % 2, 1, at_im]
            g_re = p_re * q_re + p_im * q_im
            g_im = p_im * q_re - p_re * q_im
            gain_ref[i, :, re] = g_re
            gain_ref[i, :, im] = g_im
            cos_sum, sin_sum = pred_ref[own_i, :, re], pred_ref[own_i, :, im]
            rows.append(
                (
                    SCALES[f] * jnp.sum(g_re * cos_sum + g_im * sin_sum, axis=0, keepdims=True),
                    SCALES[f] * jnp.sum(g_im * cos_sum - g_re * sin_sum, axis=0, keepdims=True),
                )
            )
            curv = curv + (g_re * g_re + g_im * g_im)
        model = jnp.concatenate([r[0] for r in rows] + [r[1] for r in rows], axis=0)
        for n in range(model_ref.shape[0]):
            model_ref[n, :, pl.ds(i * BLOCK, BLOCK)] = model
    curv_ref[...] = curv[:, :128] + curv[:, 128:]


def make_model(me, pieces, stations, preds, held, peers):
    rows, columns = pieces[0].shape
    count = sum(pred.shape[0] for pred in preds)
    vmem = pl.BlockSpec(memory_space=pltpu.VMEM)
    return pl.pallas_call(
        model_kernel,
        in_specs=[pl.BlockSpec(memory_space=pltpu.SMEM)] + [vmem] * (3 + len(preds) + len(held)),
        out_specs=[vmem] * 3,
        out_shape=[
            pltpu.VMEM((count, C, WIDE), F32),
            jax.ShapeDtypeStruct((peers, 2 * F, count * BLOCK), F32),
            jax.ShapeDtypeStruct((C, 128), F32),
        ],
        scratch_shapes=[
            pltpu.VMEM((2 * columns, 2 * rows), BF16),
            pltpu.VMEM((2, 2, columns, BLOCK), F32),
        ],
        compiler_params=pltpu.CompilerParams(vmem_limit_bytes=SCOPED),
        name="model",
    )(me, *pieces, stations, *map(in_vmem, preds), *map(in_vmem, held))


def score_kernel(parts_ref, obs_ref, gain_ref, clus_ref, curv_ref, *rest):
    *tables, out_ref, weight = rest
    chunks = len(tables) // len(GROUPS)
    blocks = [
        (tables[n * chunks : (n + 1) * chunks], i) for n in range(len(GROUPS)) for i in range(GROUPS[n])
    ]

    def weigh(i):
        at = pl.ds(i * BLOCK, BLOCK)
        model = jnp.sum(parts_ref[:, :, at], axis=0)
        for f in range(F):
            re, im = pl.ds(f * BLOCK, BLOCK), pl.ds((F + f) * BLOCK, BLOCK)
            r_re = SCALES[f] * (obs_ref[0, f : f + 1, at] - model[f : f + 1, :])
            r_im = SCALES[f] * (obs_ref[1, f : f + 1, at] - model[F + f : F + f + 1, :])
            g_re, g_im = gain_ref[i, :, re], gain_ref[i, :, im]
            weight[i % 2, :, re] = (r_re * g_re + r_im * g_im).astype(BF16)
            weight[i % 2, :, im] = (r_re * g_im - r_im * g_re).astype(BF16)

    weigh(0)
    scores = [jnp.zeros((C, CHUNK), F32)] * chunks
    for i, (group, own_i) in enumerate(blocks):
        for n in range(chunks):
            scores[n] = scores[n] + jnp.dot(
                weight[i % 2], group[n][own_i], preferred_element_type=F32
            )
        if i + 1 < len(blocks):
            weigh(i + 1)
    scores = jnp.concatenate(scores, axis=1)
    hot = lax.broadcasted_iota(jnp.int32, scores.shape, 0) == clus_ref[...]
    curv = jnp.sum(curv_ref[...], axis=1, keepdims=True)
    out_ref[0:1, :] = jnp.sum(jnp.where(hot, scores, 0.0), axis=0, keepdims=True)
    out_ref[1:2, :] = jnp.sum(jnp.where(hot, curv, 0.0), axis=0, keepdims=True)


def make_scores(parts, observed, gain, clusters, curv, tables):
    comps = clusters.shape[1]
    vmem = pl.BlockSpec(memory_space=pltpu.VMEM)
    return pl.pallas_call(
        score_kernel,
        in_specs=[vmem] * (5 + len(tables)),
        out_specs=vmem,
        out_shape=jax.ShapeDtypeStruct((2, comps), F32),
        scratch_shapes=[pltpu.VMEM((2, C, WIDE), BF16)],
        compiler_params=pltpu.CompilerParams(vmem_limit_bytes=SCOPED),
        name="scores",
    )(parts, observed, in_vmem(gain), clusters, curv, *map(in_vmem, tables))


def other_core():
    return [(i, i ^ 1) for i in range(32)]


def turn_y(k):
    return [(i, (i + 8 * k) % 32) for i in range(32)]


def turn_z(k):
    return [(i, i // 8 * 8 + ((i // 2 % 4 + k) % 4) * 2 + i % 2) for i in range(32)]


def plane_groups():
    return [[2 * i + core for i in range(16)] for core in range(2)]


def permute(x, pairs):
    return lax.ppermute(x, "row", pairs)


def per_device(
    baseline_uvw, sky_positions, fluxes, clusters, stations, station_gains, gain_step, observed_vis
):
    flux_row, cluster_row = fluxes[None, :], clusters[None, :]
    peers = lax.axis_size("comp")
    me = lax.axis_index("row").astype(jnp.int32)[None]
    firsts = [sum(GROUPS[:n]) for n in range(len(GROUPS))]

    owned = station_gains + gain_step
    others = [permute(owned, turn_z(k)) for k in (1, 2, 3)]
    tables, preds = [], []
    after = owned
    for n, count in enumerate(GROUPS):
        *parts, pred, after = make_tables(
            firsts[n],
            count,
            me,
            sky_positions,
            flux_row,
            cluster_row,
            baseline_uvw,
            after,
            tables + preds,
        )
        tables += parts
        preds.append(pred)
        if n == 0:
            after = jnp.concatenate([after] + others, axis=0)
            others = [permute(after, turn_y(k)) for k in (1, 2, 3)]
    plane = jnp.concatenate([after] + others, axis=0)
    pieces = [plane, permute(plane, other_core())]
    gain, model, curv = make_model(me, pieces, stations, preds, tables, peers)
    parts = lax.all_to_all(model, "comp", 0, 0, tiled=True)
    sums = make_scores(parts, observed_vis, gain, cluster_row, curv, tables)
    sums = sums + permute(sums, other_core())
    sums = lax.all_to_all(
        jnp.broadcast_to(sums[None], (16,) + sums.shape),
        "row",
        0,
        0,
        axis_index_groups=plane_groups(),
        tiled=True,
    ).sum(0)
    return fluxes + sums[0] / sums[1]


def solution(mesh):
    return jax.shard_map(
        per_device,
        mesh=mesh,
        in_specs=(
            P(None, "row"),
            P(None, "comp"),
            P("comp"),
            P("comp"),
            P(None, "row"),
            P("row", None),
            P("row", None),
            P(None, None, "row"),
        ),
        out_specs=P("comp"),
        check_vma=False,
    )
```

```python
import functools
import math

import jax
import jax.numpy as jnp
import numpy as np
from jax import lax
from jax.experimental import pallas as pl
from jax.experimental.pallas import tpu as pltpu
from jax.sharding import PartitionSpec as P

C = 64
F = 4
BLOCK = 256
WIDE = 2 * F * BLOCK
CHUNK = 256
TILE = 16
GROUPS = (4, 3, 1)
HALVES = ((0, 1, 2),)
SCOPED = 10 << 20
F32 = jnp.float32
BF16 = jnp.bfloat16


def sine_fit():
    y = 0.5 * np.cos(np.pi * (np.arange(400) + 0.5) / 400)
    fit = np.polynomial.polynomial.polyfit(y * y, 2.0 * np.sin(0.5 * np.pi * y) / y, 2)
    return [float(np.float32(v)) for v in fit]


ODD = sine_fit()
SCALES = (0.5, 0.25, 0.25, 0.25)
ROUND = 12582912.0


def split3(x):
    high = x.astype(BF16).astype(F32)
    rest = x - high
    mid = rest.astype(BF16).astype(F32)
    return high, mid, rest - mid


def left_terms(x):
    h, m, l = split3(x)
    return [h, h, m, h, l, m, m, l]


def right_terms(x):
    h, m, l = split3(x)
    return [h, m, h, l, h, m, l, m]


def stack_terms(terms):
    pad = jnp.zeros((8, terms[0].shape[1]), F32)
    return jnp.concatenate(terms + [pad], axis=0)


def phases(eighth):
    y = eighth - (jnp.round(eighth))
    y2 = y * y
    s = y * (ODD[0] + y2 * (ODD[1] + y2 * ODD[2]))
    cc = 4.0 - s * s
    s = s * (cc * lax.rsqrt(cc))
    c = cc - 2.0

    def double(c, s):
        return c * c - 2.0, s * c

    c1, s1 = double(c, s)
    c, s = double(c1, s1)
    c, s = double(c, s)
    c8, s8 = double(c, s)
    c9, s9 = c8 * c1 - s8 * s1, s8 * c1 + c8 * s1
    c10, s10 = c1 * c9 - (c8 + c8), c1 * s9 - (s8 + s8)
    c11, s11 = c1 * c10 - c9, c1 * s10 - s9
    return (c8, c9, c10, c11, s8, s9, s10, s11)


def table_kernel(first, count, me_ref, sky_ref, flux_ref, clus_ref, uvw_ref, pass_ref, *rest):
    *rest, sky, flux, clus, uvw_all, arrived = rest
    *table_refs, pred_ref, passed, place_ref, hot = rest[-(sky_ref.shape[1] // CHUNK + 4) :]
    if first == 0:
        sources, copies = (sky_ref, flux_ref, clus_ref, uvw_ref), (sky, flux, clus, uvw_all)
        moves = [
            pltpu.make_async_copy(source, copy, arrived.at[n])
            for n, (source, copy) in enumerate(zip(sources, copies))
        ]
        for move in moves:
            move.start()
        for move in moves:
            move.wait()
        sky_ref, flux_ref, clus_ref, uvw_ref = copies
    passed[...] = pass_ref[0 : passed.shape[0], :]
    comps = sky_ref.shape[1]
    chunks, tiles, pieces = comps // CHUNK, BLOCK // TILE, WIDE // BLOCK

    east, north = sky_ref[0:1, :], sky_ref[1:2, :]
    depth = jnp.sqrt(1.0 - east * east - north * north) - 1.0
    place = jnp.concatenate([east, north, depth], axis=0)
    place_ref[...] = stack_terms(left_terms(place)).astype(BF16)
    ids = lax.broadcasted_iota(jnp.int32, (C, comps), 0)
    hot[...] = jnp.where(ids == clus_ref[...], flux_ref[...], 0.0).astype(BF16)
    dims = (((1,), (1,)), ((), ()))

    def matmul(i, n):
        to = pl.ds(n * BLOCK, BLOCK)
        part = jnp.zeros((C, BLOCK), F32)
        for chunk in range(chunks):
            part = part + lax.dot_general(
                hot[:, pl.ds(chunk * CHUNK, CHUNK)],
                table_refs[chunk][i, to, :],
                dims,
                preferred_element_type=F32,
            )
        pred_ref[i, :, to] = part

    for i in range(count):
        uvw = uvw_ref[:, pl.ds((i + first) * BLOCK, BLOCK)]
        baseline = jnp.transpose(stack_terms(right_terms(uvw * 0.125))).astype(BF16)
        for chunk in range(chunks):
            base = jnp.dot(
                baseline, place_ref[:, pl.ds(chunk * CHUNK, CHUNK)], preferred_element_type=F32
            )
            for tile in range(tiles):
                values = phases(base[tile * TILE : (tile + 1) * TILE, :])
                for j, value in enumerate(values):
                    to = pl.ds(j * BLOCK + tile * TILE, TILE)
                    table_refs[chunk][i, to, :] = value.astype(BF16)
                done = chunk * tiles + tile
                each = chunks * tiles // pieces
                if i and done % each == each - 1:
                    matmul(i - 1, done // each)
    for n in range(pieces):
        matmul(count - 1, n)


def in_vmem(x):
    return pltpu.with_memory_space_constraint(x, pltpu.VMEM)


def make_tables(first, count, me, sky, fluxes, clusters, uvw, after, passed, held):
    comps = sky.shape[1]
    vmem = pl.BlockSpec(memory_space=pltpu.VMEM)
    chunks = comps // CHUNK
    inputs = (sky, fluxes, clusters, uvw)
    if first == 0:
        inputs = tuple(pltpu.with_memory_space_constraint(x, pltpu.HBM) for x in inputs)
    place = pl.BlockSpec(memory_space=pltpu.HBM) if first == 0 else vmem
    return pl.pallas_call(
        functools.partial(table_kernel, first, count),
        in_specs=[pl.BlockSpec(memory_space=pltpu.SMEM)] + [place] * 4 + [vmem] * (1 + len(held)),
        out_specs=[vmem] * (chunks + 2),
        out_shape=[pltpu.VMEM((count, WIDE, CHUNK), BF16)] * chunks
        + [
            pltpu.VMEM((count, C, WIDE), F32),
            jax.ShapeDtypeStruct((passed, after.shape[1]), F32),
        ],
        scratch_shapes=[
            pltpu.VMEM((32, comps), BF16),
            pltpu.VMEM((C, comps), BF16),
            *(pltpu.VMEM(x.shape, x.dtype) for x in inputs),
            pltpu.SemaphoreType.DMA((4,)),
        ],
        compiler_params=pltpu.CompilerParams(vmem_limit_bytes=SCOPED),
        cost_estimate=pl.CostEstimate(
            flops=2 * C * comps * count * WIDE,
            bytes_accessed=2 * comps * count * WIDE,
            transcendentals=4 * comps * count * WIDE,
        ),
        name="tables",
    )(me, *inputs, after, *map(in_vmem, held))


def model_kernel(first, counts, build, me_ref, *rest):
    if build:
        pieces, (pair_ref, *rest) = rest[:2], rest[2:]
        gain_ref, model_ref, curv_ref, table, found = rest[-5:]
        owned = pieces[0].shape[0] // 16
        for n, piece in enumerate(pieces):
            flat = jnp.transpose(piece[...])
            high = flat.astype(BF16)
            at = pl.ds(n * flat.shape[1], flat.shape[1])
            table[pl.ds(0, flat.shape[0]), at] = high
            low = (flat - high.astype(F32)).astype(BF16)
            table[pl.ds(flat.shape[0], flat.shape[0]), at] = low
    else:
        table, pair_ref, *rest = rest
        gain_ref, model_ref, curv_ref, found = rest[-4:]
        owned = table.shape[1] // 32
    preds = rest[: len(counts)]

    me = me_ref[0]
    my_y, my_z, my_core = me >> 3, (me >> 1) & 3, me & 1
    stations = table.shape[1]
    columns = table.shape[0] // 2
    ids = lax.broadcasted_iota(jnp.int32, (stations, BLOCK), 0)
    pair = pair_ref[...]
    owner, own = pair // owned, pair % owned
    y, z, core = owner >> 3, (owner >> 1) & 3, owner & 1
    slot = (((core ^ my_core) * 4 + ((my_y - y) & 3)) * 4 + ((my_z - z) & 3)) * owned + own

    def gather(i):
        for side in range(2):
            at = (first + i) * BLOCK
            hot = ids == slot[side : side + 1, at : at + BLOCK]
            hot = jnp.where(hot, 1.0, 0.0).astype(BF16)
            both = jnp.dot(table[...], hot, preferred_element_type=F32)
            found[i % 2, side] = both[:columns] + both[columns:]

    curv = jnp.zeros((C, BLOCK), F32)
    count = gain_ref.shape[0]
    gather(0)
    blocks = [(pred, i) for pred in preds for i in range(pred.shape[0])]
    for i, (pred_ref, own_i) in enumerate(blocks):
        if i + 1 < count:
            gather(i + 1)
        rows = []
        for f in range(F):
            re, im = pl.ds(f * BLOCK, BLOCK), pl.ds((F + f) * BLOCK, BLOCK)
            at_re, at_im = pl.ds(f * C, C), pl.ds((F + f) * C, C)
            p_re, p_im = found[i % 2, 0, at_re], found[i % 2, 0, at_im]
            q_re, q_im = found[i % 2, 1, at_re], found[i % 2, 1, at_im]
            g_re = p_re * q_re + p_im * q_im
            g_im = p_im * q_re - p_re * q_im
            gain_ref[i, :, re] = g_re
            gain_ref[i, :, im] = g_im
            cos_sum, sin_sum = pred_ref[own_i, :, re], pred_ref[own_i, :, im]
            rows.append(
                (
                    SCALES[f] * jnp.sum(g_re * cos_sum + g_im * sin_sum, axis=0, keepdims=True),
                    SCALES[f] * jnp.sum(g_im * cos_sum - g_re * sin_sum, axis=0, keepdims=True),
                )
            )
            curv = curv + (g_re * g_re + g_im * g_im)
        model = jnp.concatenate([r[0] for r in rows] + [r[1] for r in rows], axis=0)
        for n in range(model_ref.shape[0]):
            model_ref[n, :, pl.ds(i * BLOCK, BLOCK)] = model
    curv_ref[...] = curv[:, :128] + curv[:, 128:]


def make_model(first, me, pieces, stations, preds, held, peers):
    build = len(pieces) == 2
    columns = pieces[0].shape[1] if build else pieces[0].shape[0] // 2
    known = 2 * pieces[0].shape[0] if build else pieces[0].shape[1]
    counts = [pred.shape[0] for pred in preds]
    count = sum(counts)
    vmem = pl.BlockSpec(memory_space=pltpu.VMEM)
    table = [pltpu.VMEM((2 * columns, known), BF16)] if build else []
    return pl.pallas_call(
        functools.partial(model_kernel, first, counts, build),
        in_specs=[pl.BlockSpec(memory_space=pltpu.SMEM)]
        + [vmem] * (len(pieces) + 1 + len(preds) + len(held)),
        out_specs=[vmem] * (3 + len(table)),
        out_shape=[
            pltpu.VMEM((count, C, WIDE), F32),
            jax.ShapeDtypeStruct((peers, 2 * F, count * BLOCK), F32),
            jax.ShapeDtypeStruct((C, 128), F32),
        ]
        + table,
        scratch_shapes=[pltpu.VMEM((2, 2, columns, BLOCK), F32)],
        compiler_params=pltpu.CompilerParams(vmem_limit_bytes=SCOPED),
        cost_estimate=pl.CostEstimate(
            flops=16 * columns * known * count * BLOCK,
            bytes_accessed=16 * C * count * WIDE,
            transcendentals=0,
        ),
        name="model",
    )(
        me,
        *(pieces if build else map(in_vmem, pieces)),
        stations,
        *map(in_vmem, preds),
        *map(in_vmem, held),
    )


def score_kernel(first, counts, ends, more, parts_ref, obs_ref, gain_ref, clus_ref, *rest):
    curvs, (*tables, out_ref, weight) = rest[:ends], rest[ends:]
    earlier, tables = tables[:more], tables[more:]
    chunks = len(tables) // len(counts)
    blocks = [
        (tables[n * chunks : (n + 1) * chunks], i) for n in range(len(counts)) for i in range(counts[n])
    ]

    def weigh(i):
        at, seen = pl.ds(i * BLOCK, BLOCK), pl.ds((first + i) * BLOCK, BLOCK)
        model = jnp.sum(parts_ref[:, :, at], axis=0)
        for f in range(F):
            re, im = pl.ds(f * BLOCK, BLOCK), pl.ds((F + f) * BLOCK, BLOCK)
            r_re = SCALES[f] * (obs_ref[0, f : f + 1, seen] - model[f : f + 1, :])
            r_im = SCALES[f] * (obs_ref[1, f : f + 1, seen] - model[F + f : F + f + 1, :])
            g_re, g_im = gain_ref[i, :, re], gain_ref[i, :, im]
            weight[i % 2, :, re] = (r_re * g_re + r_im * g_im).astype(BF16)
            weight[i % 2, :, im] = (r_re * g_im - r_im * g_re).astype(BF16)

    weigh(0)
    scores = [jnp.zeros((C, CHUNK), F32)] * chunks
    for i, (group, own_i) in enumerate(blocks):
        for n in range(chunks):
            scores[n] = scores[n] + jnp.dot(
                weight[i % 2], group[n][own_i], preferred_element_type=F32
            )
        if i + 1 < len(blocks):
            weigh(i + 1)
    scores = jnp.concatenate(scores, axis=1)
    if not ends:
        out_ref[...] = scores
        return
    scores = sum([ref[...] for ref in earlier], scores)
    hot = lax.broadcasted_iota(jnp.int32, scores.shape, 0) == clus_ref[...]
    curv = jnp.sum(sum(curv[...] for curv in curvs), axis=1, keepdims=True)
    out_ref[0:1, :] = jnp.sum(jnp.where(hot, scores, 0.0), axis=0, keepdims=True)
    out_ref[1:2, :] = jnp.sum(jnp.where(hot, curv, 0.0), axis=0, keepdims=True)


def make_scores(first, parts, observed, gain, clusters, curvs, earlier, tables):
    comps = clusters.shape[1]
    chunks = comps // CHUNK
    counts = [tables[n].shape[0] for n in range(0, len(tables), chunks)]
    vmem = pl.BlockSpec(memory_space=pltpu.VMEM)
    return pl.pallas_call(
        functools.partial(score_kernel, first, counts, len(curvs), len(earlier)),
        in_specs=[vmem] * (4 + len(curvs) + len(earlier) + len(tables)),
        out_specs=vmem,
        out_shape=jax.ShapeDtypeStruct((2, comps), F32)
        if curvs
        else pltpu.VMEM((C, comps), F32),
        scratch_shapes=[pltpu.VMEM((2, C, WIDE), BF16)],
        compiler_params=pltpu.CompilerParams(vmem_limit_bytes=SCOPED),
        cost_estimate=pl.CostEstimate(
            flops=2 * C * comps * sum(counts) * WIDE,
            bytes_accessed=2 * comps * sum(counts) * WIDE,
            transcendentals=0,
        ),
        name="scores",
    )(
        parts,
        observed,
        in_vmem(gain),
        clusters,
        *curvs,
        *map(in_vmem, earlier),
        *map(in_vmem, tables),
    )


def other_core():
    return [(i, i ^ 1) for i in range(32)]


def turn_y(k):
    return [(i, (i + 8 * k) % 32) for i in range(32)]


def turn_z(k):
    return [(i, i // 8 * 8 + ((i // 2 % 4 + k) % 4) * 2 + i % 2) for i in range(32)]


def plane_groups():
    return [[2 * i + core for i in range(16)] for core in range(2)]


def permute(x, pairs):
    return lax.ppermute(x, "row", pairs)


def per_device(
    baseline_uvw, sky_positions, fluxes, clusters, stations, station_gains, gain_step, observed_vis
):
    flux_row, cluster_row = fluxes[None, :], clusters[None, :]
    peers = lax.axis_size("comp")
    me = lax.axis_index("row").astype(jnp.int32)[None]
    firsts = [sum(GROUPS[:n]) for n in range(len(GROUPS))]

    owned = station_gains + gain_step
    others = [permute(owned, turn_z(k)) for k in (1, 2, 3)]
    groups, preds = [], []
    after = owned
    for n, count in enumerate(GROUPS):
        *group, pred, passed = make_tables(
            firsts[n],
            count,
            me,
            sky_positions,
            flux_row,
            cluster_row,
            baseline_uvw,
            after,
            after.shape[0] if n < 2 else 8,
            [x for held in groups for x in held] + preds,
        )
        groups.append(group)
        preds.append(pred)
        if n == 0:
            after = jnp.concatenate([passed] + others, axis=0)
            others = [permute(after, turn_y(k)) for k in (1, 2, 3)]
        elif n == 1:
            after = jnp.concatenate([passed] + others, axis=0)
            pieces = [after, permute(after, other_core())]

    tables = [x for held in groups for x in held]
    gains, curvs, sent = [], [], []
    for half in HALVES:
        gain, model, curv, *table = make_model(
            firsts[half[0]],
            me,
            pieces,
            stations,
            [preds[n] for n in half],
            tables + gains,
            peers,
        )
        gains.append(gain)
        curvs.append(curv)
        sent.append(lax.all_to_all(model, "comp", 0, 0, tiled=True))
        pieces = table
    earlier = []
    for n, half in enumerate(HALVES):
        sums = make_scores(
            firsts[half[0]],
            sent[n],
            observed_vis,
            gains[n],
            cluster_row,
            curvs if n == len(HALVES) - 1 else [],
            earlier,
            [x for group in half for x in groups[group]],
        )
        earlier = [sums]
    sums = sums + permute(sums, other_core())
    sums = lax.all_to_all(
        jnp.broadcast_to(sums[None], (16,) + sums.shape),
        "row",
        0,
        0,
        axis_index_groups=plane_groups(),
        tiled=True,
    ).sum(0)
    return fluxes + sums[0] / sums[1]


def solution(mesh):
    return jax.shard_map(
        per_device,
        mesh=mesh,
        in_specs=(
            P(None, "row"),
            P(None, "comp"),
            P("comp"),
            P("comp"),
            P(None, "row"),
            P("row", None),
            P("row", None),
            P(None, None, "row"),
        ),
        out_specs=P("comp"),
        check_vma=False,
    )
```

```python
import functools
import math

import jax
import jax.numpy as jnp
import numpy as np
from jax import lax
from jax.experimental import pallas as pl
from jax.experimental.pallas import tpu as pltpu
from jax.sharding import PartitionSpec as P

C = 64
F = 4
BLOCK = 256
WIDE = 2 * F * BLOCK
CHUNK = 256
TILE = 16
GROUPS = (4, 3, 1)
HALVES = ((0, 1, 2),)
SCOPED = 10 << 20
F32 = jnp.float32
BF16 = jnp.bfloat16


def sine_fit():
    y = 0.5 * np.cos(np.pi * (np.arange(400) + 0.5) / 400)
    fit = np.polynomial.polynomial.polyfit(y * y, 2.0 * np.sin(0.5 * np.pi * y) / y, 2)
    return [float(np.float32(v)) for v in fit]


ODD = sine_fit()
SCALES = (0.5, 0.25, 0.25, 0.25)
ROUND = 12582912.0


def split3(x):
    high = x.astype(BF16).astype(F32)
    rest = x - high
    mid = rest.astype(BF16).astype(F32)
    return high, mid, rest - mid


def left_terms(x):
    h, m, l = split3(x)
    return [h, h, m, h, l, m, m, l]


def right_terms(x):
    h, m, l = split3(x)
    return [h, m, h, l, h, m, l, m]


def stack_terms(terms):
    pad = jnp.zeros((8, terms[0].shape[1]), F32)
    return jnp.concatenate(terms + [pad], axis=0)


def phases(eighth):
    y = eighth - (jnp.round(eighth))
    y2 = y * y
    s = y * (ODD[0] + y2 * (ODD[1] + y2 * ODD[2]))
    cc = 4.0 - s * s
    s = s * (cc * lax.rsqrt(cc))
    c = cc - 2.0

    def double(c, s):
        return c * c - 2.0, s * c

    c1, s1 = double(c, s)
    c, s = double(c1, s1)
    c, s = double(c, s)
    c8, s8 = double(c, s)
    c9, s9 = c8 * c1 - s8 * s1, s8 * c1 + c8 * s1
    c10, s10 = c1 * c9 - (c8 + c8), c1 * s9 - (s8 + s8)
    c11, s11 = c1 * c10 - c9, c1 * s10 - s9
    return (c8, c9, c10, c11, s8, s9, s10, s11)


def table_kernel(first, count, me_ref, sky_ref, flux_ref, clus_ref, uvw_ref, pass_ref, *rest):
    *rest, sky, flux, clus, uvw_all, arrived = rest
    *table_refs, pred_ref, passed, place_ref, hot = rest[-(sky_ref.shape[1] // CHUNK + 4) :]
    if first == 0:
        sources, copies = (sky_ref, flux_ref, clus_ref, uvw_ref), (sky, flux, clus, uvw_all)
        moves = [
            pltpu.make_async_copy(source, copy, arrived.at[n])
            for n, (source, copy) in enumerate(zip(sources, copies))
        ]
        for move in moves:
            move.start()
        for move in moves:
            move.wait()
        sky_ref, flux_ref, clus_ref, uvw_ref = copies
    passed[...] = pass_ref[0 : passed.shape[0], :]
    comps = sky_ref.shape[1]
    chunks, tiles, pieces = comps // CHUNK, BLOCK // TILE, WIDE // BLOCK

    east, north = sky_ref[0:1, :], sky_ref[1:2, :]
    depth = jnp.sqrt(1.0 - east * east - north * north) - 1.0
    place = jnp.concatenate([east, north, depth], axis=0)
    place_ref[...] = stack_terms(left_terms(place)).astype(BF16)
    ids = lax.broadcasted_iota(jnp.int32, (C, comps), 0)
    hot[...] = jnp.where(ids == clus_ref[...], flux_ref[...], 0.0).astype(BF16)
    dims = (((1,), (1,)), ((), ()))

    def matmul(i, n):
        to = pl.ds(n * BLOCK, BLOCK)
        part = jnp.zeros((C, BLOCK), F32)
        for chunk in range(chunks):
            part = part + lax.dot_general(
                hot[:, pl.ds(chunk * CHUNK, CHUNK)],
                table_refs[chunk][i, to, :],
                dims,
                preferred_element_type=F32,
            )
        pred_ref[i, :, to] = part

    for i in range(count):
        uvw = uvw_ref[:, pl.ds((i + first) * BLOCK, BLOCK)]
        baseline = jnp.transpose(stack_terms(right_terms(uvw * 0.125))).astype(BF16)
        for chunk in range(chunks):
            base = jnp.dot(
                baseline, place_ref[:, pl.ds(chunk * CHUNK, CHUNK)], preferred_element_type=F32
            )
            for tile in range(tiles):
                values = phases(base[tile * TILE : (tile + 1) * TILE, :])
                for j, value in enumerate(values):
                    to = pl.ds(j * BLOCK + tile * TILE, TILE)
                    table_refs[chunk][i, to, :] = value.astype(BF16)
                done = chunk * tiles + tile
                each = chunks * tiles // pieces
                if i and done % each == each - 1:
                    matmul(i - 1, done // each)
    for n in range(pieces):
        matmul(count - 1, n)


def in_vmem(x):
    return pltpu.with_memory_space_constraint(x, pltpu.VMEM)


def make_tables(first, count, me, sky, fluxes, clusters, uvw, after, passed, held):
    comps = sky.shape[1]
    vmem = pl.BlockSpec(memory_space=pltpu.VMEM)
    chunks = comps // CHUNK
    inputs = (sky, fluxes, clusters, uvw)
    if first == 0:
        inputs = tuple(pltpu.with_memory_space_constraint(x, pltpu.HBM) for x in inputs)
    place = pl.BlockSpec(memory_space=pltpu.HBM) if first == 0 else vmem
    return pl.pallas_call(
        functools.partial(table_kernel, first, count),
        in_specs=[pl.BlockSpec(memory_space=pltpu.SMEM)] + [place] * 4 + [vmem] * (1 + len(held)),
        out_specs=[vmem] * (chunks + 2),
        out_shape=[pltpu.VMEM((count, WIDE, CHUNK), BF16)] * chunks
        + [
            pltpu.VMEM((count, C, WIDE), F32),
            jax.ShapeDtypeStruct((passed, after.shape[1]), F32),
        ],
        scratch_shapes=[
            pltpu.VMEM((32, comps), BF16),
            pltpu.VMEM((C, comps), BF16),
            *(pltpu.VMEM(x.shape, x.dtype) for x in inputs),
            pltpu.SemaphoreType.DMA((4,)),
        ],
        compiler_params=pltpu.CompilerParams(vmem_limit_bytes=SCOPED),
        cost_estimate=pl.CostEstimate(
            flops=2 * C * comps * count * WIDE,
            bytes_accessed=2 * comps * count * WIDE,
            transcendentals=4 * comps * count * WIDE,
        ),
        name="tables",
    )(me, *inputs, after, *map(in_vmem, held))


def model_kernel(first, counts, build, me_ref, *rest):
    if build:
        pieces, (pair_ref, *rest) = rest[:2], rest[2:]
        gain_ref, model_ref, curv_ref, table, found = rest[-5:]
        owned = pieces[0].shape[0] // 16
        for n, piece in enumerate(pieces):
            flat = jnp.transpose(piece[...])
            table[:, pl.ds(n * flat.shape[1], flat.shape[1])] = flat.astype(BF16)
    else:
        table, pair_ref, *rest = rest
        gain_ref, model_ref, curv_ref, found = rest[-4:]
        owned = table.shape[1] // 32
    preds = rest[: len(counts)]

    me = me_ref[0]
    my_y, my_z, my_core = me >> 3, (me >> 1) & 3, me & 1
    stations = table.shape[1]
    ids = lax.broadcasted_iota(jnp.int32, (stations, BLOCK), 0)
    pair = pair_ref[...]
    owner, own = pair // owned, pair % owned
    y, z, core = owner >> 3, (owner >> 1) & 3, owner & 1
    slot = (((core ^ my_core) * 4 + ((my_y - y) & 3)) * 4 + ((my_z - z) & 3)) * owned + own

    def gather(i):
        for side in range(2):
            at = (first + i) * BLOCK
            hot = ids == slot[side : side + 1, at : at + BLOCK]
            hot = jnp.where(hot, 1.0, 0.0).astype(BF16)
            found[i % 2, side] = jnp.dot(table[...], hot, preferred_element_type=F32)

    curv = jnp.zeros((C, BLOCK), F32)
    count = gain_ref.shape[0]
    gather(0)
    blocks = [(pred, i) for pred in preds for i in range(pred.shape[0])]
    for i, (pred_ref, own_i) in enumerate(blocks):
        if i + 1 < count:
            gather(i + 1)
        rows = []
        for f in range(F):
            re, im = pl.ds(f * BLOCK, BLOCK), pl.ds((F + f) * BLOCK, BLOCK)
            at_re, at_im = pl.ds(f * C, C), pl.ds((F + f) * C, C)
            p_re, p_im = found[i % 2, 0, at_re], found[i % 2, 0, at_im]
            q_re, q_im = found[i % 2, 1, at_re], found[i % 2, 1, at_im]
            g_re = p_re * q_re + p_im * q_im
            g_im = p_im * q_re - p_re * q_im
            gain_ref[i, :, re] = g_re
            gain_ref[i, :, im] = g_im
            cos_sum, sin_sum = pred_ref[own_i, :, re], pred_ref[own_i, :, im]
            rows.append(
                (
                    SCALES[f] * jnp.sum(g_re * cos_sum + g_im * sin_sum, axis=0, keepdims=True),
                    SCALES[f] * jnp.sum(g_im * cos_sum - g_re * sin_sum, axis=0, keepdims=True),
                )
            )
            curv = curv + (g_re * g_re + g_im * g_im)
        model = jnp.concatenate([r[0] for r in rows] + [r[1] for r in rows], axis=0)
        for n in range(model_ref.shape[0]):
            model_ref[n, :, pl.ds(i * BLOCK, BLOCK)] = model
    curv_ref[...] = curv[:, :128] + curv[:, 128:]


def make_model(first, me, pieces, stations, preds, held, peers):
    build = len(pieces) == 2
    columns = pieces[0].shape[1] if build else pieces[0].shape[0]
    known = 2 * pieces[0].shape[0] if build else pieces[0].shape[1]
    counts = [pred.shape[0] for pred in preds]
    count = sum(counts)
    vmem = pl.BlockSpec(memory_space=pltpu.VMEM)
    table = [pltpu.VMEM((columns, known), BF16)] if build else []
    return pl.pallas_call(
        functools.partial(model_kernel, first, counts, build),
        in_specs=[pl.BlockSpec(memory_space=pltpu.SMEM)]
        + [vmem] * (len(pieces) + 1 + len(preds) + len(held)),
        out_specs=[vmem] * (3 + len(table)),
        out_shape=[
            pltpu.VMEM((count, C, WIDE), F32),
            jax.ShapeDtypeStruct((peers, 2 * F, count * BLOCK), F32),
            jax.ShapeDtypeStruct((C, 128), F32),
        ]
        + table,
        scratch_shapes=[pltpu.VMEM((2, 2, columns, BLOCK), F32)],
        compiler_params=pltpu.CompilerParams(vmem_limit_bytes=SCOPED),
        cost_estimate=pl.CostEstimate(
            flops=8 * columns * known * count * BLOCK,
            bytes_accessed=16 * C * count * WIDE,
            transcendentals=0,
        ),
        name="model",
    )(
        me,
        *(pieces if build else map(in_vmem, pieces)),
        stations,
        *map(in_vmem, preds),
        *map(in_vmem, held),
    )


def score_kernel(first, counts, ends, more, parts_ref, obs_ref, gain_ref, clus_ref, *rest):
    curvs, (*tables, out_ref, weight) = rest[:ends], rest[ends:]
    earlier, tables = tables[:more], tables[more:]
    chunks = len(tables) // len(counts)
    blocks = [
        (tables[n * chunks : (n + 1) * chunks], i) for n in range(len(counts)) for i in range(counts[n])
    ]

    def weigh(i):
        at, seen = pl.ds(i * BLOCK, BLOCK), pl.ds((first + i) * BLOCK, BLOCK)
        model = jnp.sum(parts_ref[:, :, at], axis=0)
        for f in range(F):
            re, im = pl.ds(f * BLOCK, BLOCK), pl.ds((F + f) * BLOCK, BLOCK)
            r_re = SCALES[f] * (obs_ref[0, f : f + 1, seen] - model[f : f + 1, :])
            r_im = SCALES[f] * (obs_ref[1, f : f + 1, seen] - model[F + f : F + f + 1, :])
            g_re, g_im = gain_ref[i, :, re], gain_ref[i, :, im]
            weight[i % 2, :, re] = (r_re * g_re + r_im * g_im).astype(BF16)
            weight[i % 2, :, im] = (r_re * g_im - r_im * g_re).astype(BF16)

    weigh(0)
    scores = [jnp.zeros((C, CHUNK), F32)] * chunks
    for i, (group, own_i) in enumerate(blocks):
        for n in range(chunks):
            scores[n] = scores[n] + jnp.dot(
                weight[i % 2], group[n][own_i], preferred_element_type=F32
            )
        if i + 1 < len(blocks):
            weigh(i + 1)
    scores = jnp.concatenate(scores, axis=1)
    if not ends:
        out_ref[...] = scores
        return
    scores = sum([ref[...] for ref in earlier], scores)
    hot = lax.broadcasted_iota(jnp.int32, scores.shape, 0) == clus_ref[...]
    curv = jnp.sum(sum(curv[...] for curv in curvs), axis=1, keepdims=True)
    out_ref[0:1, :] = jnp.sum(jnp.where(hot, scores, 0.0), axis=0, keepdims=True)
    out_ref[1:2, :] = jnp.sum(jnp.where(hot, curv, 0.0), axis=0, keepdims=True)


def make_scores(first, parts, observed, gain, clusters, curvs, earlier, tables):
    comps = clusters.shape[1]
    chunks = comps // CHUNK
    counts = [tables[n].shape[0] for n in range(0, len(tables), chunks)]
    vmem = pl.BlockSpec(memory_space=pltpu.VMEM)
    return pl.pallas_call(
        functools.partial(score_kernel, first, counts, len(curvs), len(earlier)),
        in_specs=[vmem] * (4 + len(curvs) + len(earlier) + len(tables)),
        out_specs=vmem,
        out_shape=jax.ShapeDtypeStruct((2, comps), F32)
        if curvs
        else pltpu.VMEM((C, comps), F32),
        scratch_shapes=[pltpu.VMEM((2, C, WIDE), BF16)],
        compiler_params=pltpu.CompilerParams(vmem_limit_bytes=SCOPED),
        cost_estimate=pl.CostEstimate(
            flops=2 * C * comps * sum(counts) * WIDE,
            bytes_accessed=2 * comps * sum(counts) * WIDE,
            transcendentals=0,
        ),
        name="scores",
    )(
        parts,
        observed,
        in_vmem(gain),
        clusters,
        *curvs,
        *map(in_vmem, earlier),
        *map(in_vmem, tables),
    )


def other_core():
    return [(i, i ^ 1) for i in range(32)]


def turn_y(k):
    return [(i, (i + 8 * k) % 32) for i in range(32)]


def turn_z(k):
    return [(i, i // 8 * 8 + ((i // 2 % 4 + k) % 4) * 2 + i % 2) for i in range(32)]


def plane_groups():
    return [[2 * i + core for i in range(16)] for core in range(2)]


def permute(x, pairs):
    return lax.ppermute(x, "row", pairs)


def per_device(
    baseline_uvw, sky_positions, fluxes, clusters, stations, station_gains, gain_step, observed_vis
):
    flux_row, cluster_row = fluxes[None, :], clusters[None, :]
    peers = lax.axis_size("comp")
    me = lax.axis_index("row").astype(jnp.int32)[None]
    firsts = [sum(GROUPS[:n]) for n in range(len(GROUPS))]

    owned = station_gains + gain_step
    others = [permute(owned, turn_z(k)) for k in (1, 2, 3)]
    groups, preds = [], []
    after = owned
    for n, count in enumerate(GROUPS):
        *group, pred, passed = make_tables(
            firsts[n],
            count,
            me,
            sky_positions,
            flux_row,
            cluster_row,
            baseline_uvw,
            after,
            after.shape[0] if n < 2 else 8,
            [x for held in groups for x in held] + preds,
        )
        groups.append(group)
        preds.append(pred)
        if n == 0:
            after = jnp.concatenate([passed] + others, axis=0)
            others = [permute(after, turn_y(k)) for k in (1, 2, 3)]
        elif n == 1:
            after = jnp.concatenate([passed] + others, axis=0)
            pieces = [after, permute(after, other_core())]

    tables = [x for held in groups for x in held]
    gains, curvs, sent = [], [], []
    for half in HALVES:
        gain, model, curv, *table = make_model(
            firsts[half[0]],
            me,
            pieces,
            stations,
            [preds[n] for n in half],
            tables + gains,
            peers,
        )
        gains.append(gain)
        curvs.append(curv)
        sent.append(lax.all_to_all(model, "comp", 0, 0, tiled=True))
        pieces = table
    earlier = []
    for n, half in enumerate(HALVES):
        sums = make_scores(
            firsts[half[0]],
            sent[n],
            observed_vis,
            gains[n],
            cluster_row,
            curvs if n == len(HALVES) - 1 else [],
            earlier,
            [x for group in half for x in groups[group]],
        )
        earlier = [sums]
    sums = sums + permute(sums, other_core())
    sums = lax.all_to_all(
        jnp.broadcast_to(sums[None], (16,) + sums.shape),
        "row",
        0,
        0,
        axis_index_groups=plane_groups(),
        tiled=True,
    ).sum(0)
    return fluxes + sums[0] / sums[1]


def solution(mesh):
    return jax.shard_map(
        per_device,
        mesh=mesh,
        in_specs=(
            P(None, "row"),
            P(None, "comp"),
            P("comp"),
            P("comp"),
            P(None, "row"),
            P("row", None),
            P("row", None),
            P(None, None, "row"),
        ),
        out_specs=P("comp"),
        check_vma=False,
    )
```

```python
import functools
import math

import jax
import jax.numpy as jnp
import numpy as np
from jax import lax
from jax.experimental import pallas as pl
from jax.experimental.pallas import tpu as pltpu
from jax.sharding import PartitionSpec as P

C = 64
F = 4
BLOCK = 256
WIDE = 2 * F * BLOCK
CHUNK = 256
TILE = 16
GROUPS = (4, 3, 1)
HALVES = ((0, 1, 2),)
SCOPED = 10 << 20
F32 = jnp.float32
BF16 = jnp.bfloat16


def sine_fit():
    y = 0.5 * np.cos(np.pi * (np.arange(400) + 0.5) / 400)
    fit = np.polynomial.polynomial.polyfit(y * y, 2.0 * np.sin(0.5 * np.pi * y) / y, 2)
    return [float(np.float32(v)) for v in fit]


ODD = sine_fit()
SCALES = (0.5, 0.25, 0.25, 0.25)
ROUND = 12582912.0


def split3(x):
    high = x.astype(BF16).astype(F32)
    rest = x - high
    mid = rest.astype(BF16).astype(F32)
    return high, mid, rest - mid


def left_terms(x):
    h, m, l = split3(x)
    return [h, h, m, h, l, m, m, l]


def right_terms(x):
    h, m, l = split3(x)
    return [h, m, h, l, h, m, l, m]


def stack_terms(terms):
    pad = jnp.zeros((8, terms[0].shape[1]), F32)
    return jnp.concatenate(terms + [pad], axis=0)


def phases(eighth):
    y = eighth - (jnp.round(eighth))
    y2 = y * y
    s = y * (ODD[0] + y2 * (ODD[1] + y2 * ODD[2]))
    cc = 4.0 - s * s
    s = s * (cc * lax.rsqrt(cc))
    c = cc - 2.0

    def double(c, s):
        return c * c - 2.0, s * c

    c1, s1 = double(c, s)
    c, s = double(c1, s1)
    c, s = double(c, s)
    c8, s8 = double(c, s)
    c9, s9 = c8 * c1 - s8 * s1, s8 * c1 + c8 * s1
    c10, s10 = c1 * c9 - (c8 + c8), c1 * s9 - (s8 + s8)
    c11, s11 = c1 * c10 - c9, c1 * s10 - s9
    return (c8, c9, c10, c11, s8, s9, s10, s11)


def table_kernel(first, count, me_ref, sky_ref, flux_ref, clus_ref, uvw_ref, pass_ref, *rest):
    *rest, sky, flux, clus, uvw_all, arrived = rest
    *table_refs, pred_ref, passed, place_ref, hot = rest[-(sky_ref.shape[1] // CHUNK + 4) :]
    if first == 0:
        sources, copies = (sky_ref, flux_ref, clus_ref, uvw_ref), (sky, flux, clus, uvw_all)
        moves = [
            pltpu.make_async_copy(source, copy, arrived.at[n])
            for n, (source, copy) in enumerate(zip(sources, copies))
        ]
        for move in moves:
            move.start()
        for move in moves:
            move.wait()
        sky_ref, flux_ref, clus_ref, uvw_ref = copies
    passed[...] = pass_ref[0 : passed.shape[0], :]
    comps = sky_ref.shape[1]
    chunks, tiles, pieces = comps // CHUNK, BLOCK // TILE, WIDE // BLOCK

    east, north = sky_ref[0:1, :], sky_ref[1:2, :]
    depth = jnp.sqrt(1.0 - east * east - north * north) - 1.0
    place = jnp.concatenate([east, north, depth], axis=0)
    place_ref[...] = stack_terms(left_terms(place)).astype(BF16)
    ids = lax.broadcasted_iota(jnp.int32, (C, comps), 0)
    hot[...] = jnp.where(ids == clus_ref[...], flux_ref[...], 0.0).astype(BF16)
    dims = (((1,), (1,)), ((), ()))

    def matmul(i, n):
        to = pl.ds(n * BLOCK, BLOCK)
        part = jnp.zeros((C, BLOCK), F32)
        for chunk in range(chunks):
            part = part + lax.dot_general(
                hot[:, pl.ds(chunk * CHUNK, CHUNK)],
                table_refs[chunk][i, to, :],
                dims,
                preferred_element_type=F32,
            )
        pred_ref[i, :, to] = part

    for i in range(count):
        uvw = uvw_ref[:, pl.ds((i + first) * BLOCK, BLOCK)]
        baseline = jnp.transpose(stack_terms(right_terms(uvw * 0.125))).astype(BF16)
        for chunk in range(chunks):
            base = jnp.dot(
                baseline, place_ref[:, pl.ds(chunk * CHUNK, CHUNK)], preferred_element_type=F32
            )
            for tile in range(tiles):
                values = phases(base[tile * TILE : (tile + 1) * TILE, :])
                for j, value in enumerate(values):
                    to = pl.ds(j * BLOCK + tile * TILE, TILE)
                    table_refs[chunk][i, to, :] = value.astype(BF16)
                done = chunk * tiles + tile
                each = chunks * tiles // pieces
                if i and done % each == each - 1:
                    matmul(i - 1, done // each)
    for n in range(pieces):
        matmul(count - 1, n)


def in_vmem(x):
    return pltpu.with_memory_space_constraint(x, pltpu.VMEM)


def make_tables(first, count, me, sky, fluxes, clusters, uvw, after, passed, held):
    comps = sky.shape[1]
    vmem = pl.BlockSpec(memory_space=pltpu.VMEM)
    chunks = comps // CHUNK
    inputs = (sky, fluxes, clusters, uvw)
    if first == 0:
        inputs = tuple(pltpu.with_memory_space_constraint(x, pltpu.HBM) for x in inputs)
    place = pl.BlockSpec(memory_space=pltpu.HBM) if first == 0 else vmem
    return pl.pallas_call(
        functools.partial(table_kernel, first, count),
        in_specs=[pl.BlockSpec(memory_space=pltpu.SMEM)] + [place] * 4 + [vmem] * (1 + len(held)),
        out_specs=[vmem] * (chunks + 2),
        out_shape=[pltpu.VMEM((count, WIDE, CHUNK), BF16)] * chunks
        + [
            pltpu.VMEM((count, C, WIDE), F32),
            jax.ShapeDtypeStruct((passed, after.shape[1]), F32),
        ],
        scratch_shapes=[
            pltpu.VMEM((32, comps), BF16),
            pltpu.VMEM((C, comps), BF16),
            *(pltpu.VMEM(x.shape, x.dtype) for x in inputs),
            pltpu.SemaphoreType.DMA((4,)),
        ],
        compiler_params=pltpu.CompilerParams(vmem_limit_bytes=SCOPED),
        cost_estimate=pl.CostEstimate(
            flops=2 * C * comps * count * WIDE,
            bytes_accessed=2 * comps * count * WIDE,
            transcendentals=4 * comps * count * WIDE,
        ),
        name="tables",
    )(me, *inputs, after, *map(in_vmem, held))


def model_kernel(first, counts, build, me_ref, *rest):
    if build:
        pieces, (pair_ref, *rest) = rest[:2], rest[2:]
        gain_ref, model_ref, curv_ref, table, found = rest[-5:]
        owned = pieces[0].shape[0] // 16
        for n, piece in enumerate(pieces):
            flat = jnp.transpose(piece[...])
            table[:, pl.ds(n * flat.shape[1], flat.shape[1])] = flat.astype(BF16)
    else:
        table, pair_ref, *rest = rest
        gain_ref, model_ref, curv_ref, found = rest[-4:]
        owned = table.shape[1] // 32
    preds = rest[: len(counts)]

    me = me_ref[0]
    my_y, my_z, my_core = me >> 3, (me >> 1) & 3, me & 1
    stations = table.shape[1]
    ids = lax.broadcasted_iota(jnp.int32, (stations, BLOCK), 0)
    pair = pair_ref[...]
    owner, own = pair // owned, pair % owned
    y, z, core = owner >> 3, (owner >> 1) & 3, owner & 1
    slot = (((core ^ my_core) * 4 + ((my_y - y) & 3)) * 4 + ((my_z - z) & 3)) * owned + own

    def gather(i):
        for side in range(2):
            at = (first + i) * BLOCK
            hot = ids == slot[side : side + 1, at : at + BLOCK]
            hot = jnp.where(hot, 1.0, 0.0).astype(BF16)
            found[i % 2, side] = jnp.dot(table[...], hot, preferred_element_type=F32)

    curv = jnp.zeros((C, BLOCK), F32)
    count = gain_ref.shape[0]
    gather(0)
    blocks = [(pred, i) for pred in preds for i in range(pred.shape[0])]
    for i, (pred_ref, own_i) in enumerate(blocks):
        if i + 1 < count:
            gather(i + 1)
        rows = []
        for f in range(F):
            re, im = pl.ds(f * BLOCK, BLOCK), pl.ds((F + f) * BLOCK, BLOCK)
            at_re, at_im = pl.ds(f * C, C), pl.ds((F + f) * C, C)
            p_re, p_im = found[i % 2, 0, at_re], found[i % 2, 0, at_im]
            q_re, q_im = found[i % 2, 1, at_re], found[i % 2, 1, at_im]
            g_re = p_re * q_re + p_im * q_im
            g_im = p_im * q_re - p_re * q_im
            gain_ref[i, :, re] = g_re
            gain_ref[i, :, im] = g_im
            cos_sum, sin_sum = pred_ref[own_i, :, re], pred_ref[own_i, :, im]
            rows.append(
                (
                    SCALES[f] * jnp.sum(g_re * cos_sum + g_im * sin_sum, axis=0, keepdims=True),
                    SCALES[f] * jnp.sum(g_im * cos_sum - g_re * sin_sum, axis=0, keepdims=True),
                )
            )
            curv = curv + (g_re * g_re + g_im * g_im)
        model = jnp.concatenate([r[0] for r in rows] + [r[1] for r in rows], axis=0)
        for n in range(model_ref.shape[0]):
            model_ref[n, :, pl.ds(i * BLOCK, BLOCK)] = model
    curv_ref[...] = curv[:, :128] + curv[:, 128:]


def make_model(first, me, pieces, stations, preds, held, peers):
    build = len(pieces) == 2
    columns = pieces[0].shape[1] if build else pieces[0].shape[0]
    known = 2 * pieces[0].shape[0] if build else pieces[0].shape[1]
    counts = [pred.shape[0] for pred in preds]
    count = sum(counts)
    vmem = pl.BlockSpec(memory_space=pltpu.VMEM)
    table = [pltpu.VMEM((columns, known), BF16)] if build else []
    return pl.pallas_call(
        functools.partial(model_kernel, first, counts, build),
        in_specs=[pl.BlockSpec(memory_space=pltpu.SMEM)]
        + [vmem] * (len(pieces) + 1 + len(preds) + len(held)),
        out_specs=[vmem] * (3 + len(table)),
        out_shape=[
            pltpu.VMEM((count, C, WIDE), F32),
            jax.ShapeDtypeStruct((peers, 2 * F, count * BLOCK), F32),
            jax.ShapeDtypeStruct((C, 128), F32),
        ]
        + table,
        scratch_shapes=[pltpu.VMEM((2, 2, columns, BLOCK), F32)],
        compiler_params=pltpu.CompilerParams(vmem_limit_bytes=SCOPED),
        cost_estimate=pl.CostEstimate(
            flops=8 * columns * known * count * BLOCK,
            bytes_accessed=16 * C * count * WIDE,
            transcendentals=0,
        ),
        name="model",
    )(
        me,
        *(pieces if build else map(in_vmem, pieces)),
        stations,
        *map(in_vmem, preds),
        *map(in_vmem, held),
    )


def score_kernel(first, counts, ends, more, parts_ref, obs_ref, gain_ref, clus_ref, *rest):
    curvs, (*tables, out_ref, weight) = rest[:ends], rest[ends:]
    earlier, tables = tables[:more], tables[more:]
    chunks = len(tables) // len(counts)
    blocks = [
        (tables[n * chunks : (n + 1) * chunks], i) for n in range(len(counts)) for i in range(counts[n])
    ]

    def weigh(i):
        at, seen = pl.ds(i * BLOCK, BLOCK), pl.ds((first + i) * BLOCK, BLOCK)
        model = jnp.sum(parts_ref[:, :, at], axis=0)
        for f in range(F):
            re, im = pl.ds(f * BLOCK, BLOCK), pl.ds((F + f) * BLOCK, BLOCK)
            r_re = SCALES[f] * (obs_ref[0, f : f + 1, seen] - model[f : f + 1, :])
            r_im = SCALES[f] * (obs_ref[1, f : f + 1, seen] - model[F + f : F + f + 1, :])
            g_re, g_im = gain_ref[i, :, re], gain_ref[i, :, im]
            weight[i % 2, :, re] = (r_re * g_re + r_im * g_im).astype(BF16)
            weight[i % 2, :, im] = (r_re * g_im - r_im * g_re).astype(BF16)

    weigh(0)
    scores = [jnp.zeros((C, CHUNK), F32)] * chunks
    for i, (group, own_i) in enumerate(blocks):
        for n in range(chunks):
            scores[n] = scores[n] + jnp.dot(
                weight[i % 2], group[n][own_i], preferred_element_type=F32
            )
        if i + 1 < len(blocks):
            weigh(i + 1)
    scores = jnp.concatenate(scores, axis=1)
    if not ends:
        out_ref[...] = scores
        return
    scores = sum([ref[...] for ref in earlier], scores)
    hot = lax.broadcasted_iota(jnp.int32, scores.shape, 0) == clus_ref[...]
    comps = scores.shape[1]
    curv = sum(curv[...] for curv in curvs)
    curv = jnp.concatenate([curv, jnp.zeros_like(curv)], axis=0)
    out_ref[:, 0:comps] = jnp.sum(jnp.where(hot, scores, 0.0), axis=0, keepdims=True)
    out_ref[:, comps : comps + 128] = jnp.sum(jnp.transpose(curv), axis=0, keepdims=True)


def flux_kernel(parts_ref, flux_ref, clus_ref, out_ref):
    total = jnp.sum(parts_ref[...], axis=0)
    comps = flux_ref.shape[1]
    curv = jnp.transpose(jnp.broadcast_to(total[:, comps:], (128, 128)))[0:C, 0:1]
    hot = lax.broadcasted_iota(jnp.int32, (C, comps), 0) == clus_ref[...]
    curv = jnp.sum(jnp.where(hot, curv, 0.0), axis=0, keepdims=True)
    out_ref[...] = flux_ref[...] + total[:, 0:comps] / curv


def make_scores(first, parts, observed, gain, clusters, curvs, earlier, tables):
    comps = clusters.shape[1]
    chunks = comps // CHUNK
    counts = [tables[n].shape[0] for n in range(0, len(tables), chunks)]
    vmem = pl.BlockSpec(memory_space=pltpu.VMEM)
    return pl.pallas_call(
        functools.partial(score_kernel, first, counts, len(curvs), len(earlier)),
        in_specs=[vmem] * (4 + len(curvs) + len(earlier) + len(tables)),
        out_specs=vmem,
        out_shape=jax.ShapeDtypeStruct((1, comps + 128), F32)
        if curvs
        else pltpu.VMEM((C, comps), F32),
        scratch_shapes=[pltpu.VMEM((2, C, WIDE), BF16)],
        compiler_params=pltpu.CompilerParams(vmem_limit_bytes=SCOPED),
        cost_estimate=pl.CostEstimate(
            flops=2 * C * comps * sum(counts) * WIDE,
            bytes_accessed=2 * comps * sum(counts) * WIDE,
            transcendentals=0,
        ),
        name="scores",
    )(
        parts,
        observed,
        in_vmem(gain),
        clusters,
        *curvs,
        *map(in_vmem, earlier),
        *map(in_vmem, tables),
    )


def other_core():
    return [(i, i ^ 1) for i in range(32)]


def turn_y(k):
    return [(i, (i + 8 * k) % 32) for i in range(32)]


def turn_z(k):
    return [(i, i // 8 * 8 + ((i // 2 % 4 + k) % 4) * 2 + i % 2) for i in range(32)]


def plane_groups():
    return [[2 * i + core for i in range(16)] for core in range(2)]


def permute(x, pairs):
    return lax.ppermute(x, "row", pairs)


def per_device(
    baseline_uvw, sky_positions, fluxes, clusters, stations, station_gains, gain_step, observed_vis
):
    flux_row, cluster_row = fluxes[None, :], clusters[None, :]
    peers = lax.axis_size("comp")
    me = lax.axis_index("row").astype(jnp.int32)[None]
    firsts = [sum(GROUPS[:n]) for n in range(len(GROUPS))]

    owned = station_gains + gain_step
    others = [permute(owned, turn_z(k)) for k in (1, 2, 3)]
    groups, preds = [], []
    after = owned
    for n, count in enumerate(GROUPS):
        *group, pred, passed = make_tables(
            firsts[n],
            count,
            me,
            sky_positions,
            flux_row,
            cluster_row,
            baseline_uvw,
            after,
            after.shape[0] if n < 2 else 8,
            [x for held in groups for x in held] + preds,
        )
        groups.append(group)
        preds.append(pred)
        if n == 0:
            after = jnp.concatenate([passed] + others, axis=0)
            others = [permute(after, turn_y(k)) for k in (1, 2, 3)]
        elif n == 1:
            after = jnp.concatenate([passed] + others, axis=0)
            pieces = [after, permute(after, other_core())]

    tables = [x for held in groups for x in held]
    gains, curvs, sent = [], [], []
    for half in HALVES:
        gain, model, curv, *table = make_model(
            firsts[half[0]],
            me,
            pieces,
            stations,
            [preds[n] for n in half],
            tables + gains,
            peers,
        )
        gains.append(gain)
        curvs.append(curv)
        sent.append(lax.all_to_all(model, "comp", 0, 0, tiled=True))
        pieces = table
    earlier = []
    for n, half in enumerate(HALVES):
        sums = make_scores(
            firsts[half[0]],
            sent[n],
            observed_vis,
            gains[n],
            cluster_row,
            curvs if n == len(HALVES) - 1 else [],
            earlier,
            [x for group in half for x in groups[group]],
        )
        earlier = [sums]
    sums = sums + permute(sums, other_core())
    sums = lax.all_to_all(
        jnp.broadcast_to(sums[None], (16,) + sums.shape),
        "row",
        0,
        0,
        axis_index_groups=plane_groups(),
        tiled=True,
    )
    return pl.pallas_call(
        flux_kernel, out_shape=jax.ShapeDtypeStruct(flux_row.shape, F32), name="flux"
    )(sums, flux_row, cluster_row)[0]


def solution(mesh):
    return jax.shard_map(
        per_device,
        mesh=mesh,
        in_specs=(
            P(None, "row"),
            P(None, "comp"),
            P("comp"),
            P("comp"),
            P(None, "row"),
            P("row", None),
            P("row", None),
            P(None, None, "row"),
        ),
        out_specs=P("comp"),
        check_vma=False,
    )
```

```python
import functools
import math

import jax
import jax.numpy as jnp
import numpy as np
from jax import lax
from jax.experimental import pallas as pl
from jax.experimental.pallas import tpu as pltpu
from jax.sharding import PartitionSpec as P

C = 64
F = 4
BLOCK = 256
WIDE = 2 * F * BLOCK
CHUNK = 256
TILE = 16
GROUPS = (4, 4)
HALVES = ((0, 1),)
SCOPED = 10 << 20
F32 = jnp.float32
BF16 = jnp.bfloat16


def sine_fit():
    y = 0.5 * np.cos(np.pi * (np.arange(400) + 0.5) / 400)
    fit = np.polynomial.polynomial.polyfit(y * y, 2.0 * np.sin(0.5 * np.pi * y) / y, 2)
    return [float(np.float32(v)) for v in fit]


ODD = sine_fit()
SCALES = (0.5, 0.25, 0.25, 0.25)
ROUND = 12582912.0


def split3(x):
    high = x.astype(BF16).astype(F32)
    rest = x - high
    mid = rest.astype(BF16).astype(F32)
    return high, mid, rest - mid


def left_terms(x):
    h, m, l = split3(x)
    return [h, h, m, h, l, m, m, l]


def right_terms(x):
    h, m, l = split3(x)
    return [h, m, h, l, h, m, l, m]


def stack_terms(terms):
    pad = jnp.zeros((8, terms[0].shape[1]), F32)
    return jnp.concatenate(terms + [pad], axis=0)


def phases(eighth):
    y = eighth - (jnp.round(eighth))
    y2 = y * y
    s = y * (ODD[0] + y2 * (ODD[1] + y2 * ODD[2]))
    cc = 4.0 - s * s
    s = s * (cc * lax.rsqrt(cc))
    c = cc - 2.0

    def double(c, s):
        return c * c - 2.0, s * c

    c1, s1 = double(c, s)
    c, s = double(c1, s1)
    c, s = double(c, s)
    c8, s8 = double(c, s)
    c9, s9 = c8 * c1 - s8 * s1, s8 * c1 + c8 * s1
    c10, s10 = c1 * c9 - (c8 + c8), c1 * s9 - (s8 + s8)
    c11, s11 = c1 * c10 - c9, c1 * s10 - s9
    return (c8, c9, c10, c11, s8, s9, s10, s11)


def table_kernel(first, count, me_ref, sky_ref, flux_ref, clus_ref, uvw_ref, pass_ref, *rest):
    *rest, sky, flux, clus, uvw_all, arrived = rest
    *table_refs, pred_ref, passed, place_ref, hot = rest[-(sky_ref.shape[1] // CHUNK + 4) :]
    if first == 0:
        sources, copies = (sky_ref, flux_ref, clus_ref, uvw_ref), (sky, flux, clus, uvw_all)
        moves = [
            pltpu.make_async_copy(source, copy, arrived.at[n])
            for n, (source, copy) in enumerate(zip(sources, copies))
        ]
        for move in moves:
            move.start()
        for move in moves:
            move.wait()
        sky_ref, flux_ref, clus_ref, uvw_ref = copies
    passed[...] = pass_ref[0 : passed.shape[0], :]
    comps = sky_ref.shape[1]
    chunks, tiles, pieces = comps // CHUNK, BLOCK // TILE, WIDE // BLOCK

    east, north = sky_ref[0:1, :], sky_ref[1:2, :]
    depth = jnp.sqrt(1.0 - east * east - north * north) - 1.0
    place = jnp.concatenate([east, north, depth], axis=0)
    place_ref[...] = stack_terms(left_terms(place)).astype(BF16)
    ids = lax.broadcasted_iota(jnp.int32, (C, comps), 0)
    hot[...] = jnp.where(ids == clus_ref[...], flux_ref[...], 0.0).astype(BF16)
    dims = (((1,), (1,)), ((), ()))

    def matmul(i, n):
        to = pl.ds(n * BLOCK, BLOCK)
        part = jnp.zeros((C, BLOCK), F32)
        for chunk in range(chunks):
            part = part + lax.dot_general(
                hot[:, pl.ds(chunk * CHUNK, CHUNK)],
                table_refs[chunk][i, to, :],
                dims,
                preferred_element_type=F32,
            )
        pred_ref[i, :, to] = part

    for i in range(count):
        uvw = uvw_ref[:, pl.ds((i + first) * BLOCK, BLOCK)]
        baseline = jnp.transpose(stack_terms(right_terms(uvw * 0.125))).astype(BF16)
        for chunk in range(chunks):
            base = jnp.dot(
                baseline, place_ref[:, pl.ds(chunk * CHUNK, CHUNK)], preferred_element_type=F32
            )
            for tile in range(tiles):
                values = phases(base[tile * TILE : (tile + 1) * TILE, :])
                for j, value in enumerate(values):
                    to = pl.ds(j * BLOCK + tile * TILE, TILE)
                    table_refs[chunk][i, to, :] = value.astype(BF16)
                done = chunk * tiles + tile
                each = chunks * tiles // pieces
                if i and done % each == each - 1:
                    matmul(i - 1, done // each)
    for n in range(pieces):
        matmul(count - 1, n)


def in_vmem(x):
    return pltpu.with_memory_space_constraint(x, pltpu.VMEM)


def make_tables(first, count, me, sky, fluxes, clusters, uvw, after, passed, held):
    comps = sky.shape[1]
    vmem = pl.BlockSpec(memory_space=pltpu.VMEM)
    chunks = comps // CHUNK
    inputs = (sky, fluxes, clusters, uvw)
    if first == 0:
        inputs = tuple(pltpu.with_memory_space_constraint(x, pltpu.HBM) for x in inputs)
    place = pl.BlockSpec(memory_space=pltpu.HBM) if first == 0 else vmem
    return pl.pallas_call(
        functools.partial(table_kernel, first, count),
        in_specs=[pl.BlockSpec(memory_space=pltpu.SMEM)] + [place] * 4 + [vmem] * (1 + len(held)),
        out_specs=[vmem] * (chunks + 2),
        out_shape=[pltpu.VMEM((count, WIDE, CHUNK), BF16)] * chunks
        + [
            pltpu.VMEM((count, C, WIDE), F32),
            jax.ShapeDtypeStruct((passed, after.shape[1]), F32),
        ],
        scratch_shapes=[
            pltpu.VMEM((32, comps), BF16),
            pltpu.VMEM((C, comps), BF16),
            *(pltpu.VMEM(x.shape, x.dtype) for x in inputs),
            pltpu.SemaphoreType.DMA((4,)),
        ],
        compiler_params=pltpu.CompilerParams(vmem_limit_bytes=SCOPED),
        cost_estimate=pl.CostEstimate(
            flops=2 * C * comps * count * WIDE,
            bytes_accessed=2 * comps * count * WIDE,
            transcendentals=4 * comps * count * WIDE,
        ),
        name="tables",
    )(me, *inputs, after, *map(in_vmem, held))


def model_kernel(first, counts, build, me_ref, *rest):
    if build:
        pieces, (pair_ref, *rest) = rest[:2], rest[2:]
        gain_ref, model_ref, curv_ref, table, found = rest[-5:]
        owned = pieces[0].shape[0] // 16
        for n, piece in enumerate(pieces):
            flat = jnp.transpose(piece[...])
            table[:, pl.ds(n * flat.shape[1], flat.shape[1])] = flat.astype(BF16)
    else:
        table, pair_ref, *rest = rest
        gain_ref, model_ref, curv_ref, found = rest[-4:]
        owned = table.shape[1] // 32
    preds = rest[: len(counts)]

    me = me_ref[0]
    my_y, my_z, my_core = me >> 3, (me >> 1) & 3, me & 1
    stations = table.shape[1]
    ids = lax.broadcasted_iota(jnp.int32, (stations, BLOCK), 0)
    pair = pair_ref[...]
    owner, own = pair // owned, pair % owned
    y, z, core = owner >> 3, (owner >> 1) & 3, owner & 1
    slot = (((core ^ my_core) * 4 + ((my_y - y) & 3)) * 4 + ((my_z - z) & 3)) * owned + own

    def gather(i):
        for side in range(2):
            at = (first + i) * BLOCK
            hot = ids == slot[side : side + 1, at : at + BLOCK]
            hot = jnp.where(hot, 1.0, 0.0).astype(BF16)
            found[i % 2, side] = jnp.dot(table[...], hot, preferred_element_type=F32)

    curv = jnp.zeros((C, BLOCK), F32)
    count = gain_ref.shape[0]
    gather(0)
    blocks = [(pred, i) for pred in preds for i in range(pred.shape[0])]
    for i, (pred_ref, own_i) in enumerate(blocks):
        if i + 1 < count:
            gather(i + 1)
        rows = []
        for f in range(F):
            re, im = pl.ds(f * BLOCK, BLOCK), pl.ds((F + f) * BLOCK, BLOCK)
            at_re, at_im = pl.ds(f * C, C), pl.ds((F + f) * C, C)
            p_re, p_im = found[i % 2, 0, at_re], found[i % 2, 0, at_im]
            q_re, q_im = found[i % 2, 1, at_re], found[i % 2, 1, at_im]
            g_re = p_re * q_re + p_im * q_im
            g_im = p_im * q_re - p_re * q_im
            gain_ref[i, :, re] = g_re
            gain_ref[i, :, im] = g_im
            cos_sum, sin_sum = pred_ref[own_i, :, re], pred_ref[own_i, :, im]
            rows.append(
                (
                    SCALES[f] * jnp.sum(g_re * cos_sum + g_im * sin_sum, axis=0, keepdims=True),
                    SCALES[f] * jnp.sum(g_im * cos_sum - g_re * sin_sum, axis=0, keepdims=True),
                )
            )
            curv = curv + (g_re * g_re + g_im * g_im)
        model = jnp.concatenate([r[0] for r in rows] + [r[1] for r in rows], axis=0)
        for n in range(model_ref.shape[0]):
            model_ref[n, :, pl.ds(i * BLOCK, BLOCK)] = model
    curv_ref[...] = curv[:, :128] + curv[:, 128:]


def make_model(first, me, pieces, stations, preds, held, peers):
    build = len(pieces) == 2
    columns = pieces[0].shape[1] if build else pieces[0].shape[0]
    known = 2 * pieces[0].shape[0] if build else pieces[0].shape[1]
    counts = [pred.shape[0] for pred in preds]
    count = sum(counts)
    vmem = pl.BlockSpec(memory_space=pltpu.VMEM)
    table = [pltpu.VMEM((columns, known), BF16)] if build else []
    return pl.pallas_call(
        functools.partial(model_kernel, first, counts, build),
        in_specs=[pl.BlockSpec(memory_space=pltpu.SMEM)]
        + [vmem] * (len(pieces) + 1 + len(preds) + len(held)),
        out_specs=[vmem] * (3 + len(table)),
        out_shape=[
            pltpu.VMEM((count, C, WIDE), F32),
            jax.ShapeDtypeStruct((peers, 2 * F, count * BLOCK), F32),
            jax.ShapeDtypeStruct((C, 128), F32),
        ]
        + table,
        scratch_shapes=[pltpu.VMEM((2, 2, columns, BLOCK), F32)],
        compiler_params=pltpu.CompilerParams(vmem_limit_bytes=SCOPED),
        cost_estimate=pl.CostEstimate(
            flops=8 * columns * known * count * BLOCK,
            bytes_accessed=16 * C * count * WIDE,
            transcendentals=0,
        ),
        name="model",
    )(
        me,
        *(pieces if build else map(in_vmem, pieces)),
        stations,
        *map(in_vmem, preds),
        *map(in_vmem, held),
    )


def score_kernel(first, counts, ends, more, parts_ref, obs_ref, gain_ref, clus_ref, *rest):
    curvs, (*tables, out_ref, weight) = rest[:ends], rest[ends:]
    earlier, tables = tables[:more], tables[more:]
    chunks = len(tables) // len(counts)
    blocks = [
        (tables[n * chunks : (n + 1) * chunks], i) for n in range(len(counts)) for i in range(counts[n])
    ]

    def weigh(i):
        at, seen = pl.ds(i * BLOCK, BLOCK), pl.ds((first + i) * BLOCK, BLOCK)
        model = jnp.sum(parts_ref[:, :, at], axis=0)
        for f in range(F):
            re, im = pl.ds(f * BLOCK, BLOCK), pl.ds((F + f) * BLOCK, BLOCK)
            r_re = SCALES[f] * (obs_ref[0, f : f + 1, seen] - model[f : f + 1, :])
            r_im = SCALES[f] * (obs_ref[1, f : f + 1, seen] - model[F + f : F + f + 1, :])
            g_re, g_im = gain_ref[i, :, re], gain_ref[i, :, im]
            weight[i % 2, :, re] = (r_re * g_re + r_im * g_im).astype(BF16)
            weight[i % 2, :, im] = (r_re * g_im - r_im * g_re).astype(BF16)

    weigh(0)
    scores = [jnp.zeros((C, CHUNK), F32)] * chunks
    for i, (group, own_i) in enumerate(blocks):
        for n in range(chunks):
            scores[n] = scores[n] + jnp.dot(
                weight[i % 2], group[n][own_i], preferred_element_type=F32
            )
        if i + 1 < len(blocks):
            weigh(i + 1)
    scores = jnp.concatenate(scores, axis=1)
    if not ends:
        out_ref[...] = scores
        return
    scores = sum([ref[...] for ref in earlier], scores)
    hot = lax.broadcasted_iota(jnp.int32, scores.shape, 0) == clus_ref[...]
    comps = scores.shape[1]
    curv = sum(curv[...] for curv in curvs)
    curv = jnp.concatenate([curv, jnp.zeros_like(curv)], axis=0)
    out_ref[:, 0:comps] = jnp.sum(jnp.where(hot, scores, 0.0), axis=0, keepdims=True)
    out_ref[:, comps : comps + 128] = jnp.sum(jnp.transpose(curv), axis=0, keepdims=True)


def flux_kernel(parts_ref, flux_ref, clus_ref, out_ref):
    total = jnp.sum(parts_ref[...], axis=0)
    comps = flux_ref.shape[1]
    curv = jnp.transpose(jnp.broadcast_to(total[:, comps:], (128, 128)))[0:C, 0:1]
    hot = lax.broadcasted_iota(jnp.int32, (C, comps), 0) == clus_ref[...]
    curv = jnp.sum(jnp.where(hot, curv, 0.0), axis=0, keepdims=True)
    out_ref[...] = flux_ref[...] + total[:, 0:comps] / curv


def make_scores(first, parts, observed, gain, clusters, curvs, earlier, tables):
    comps = clusters.shape[1]
    chunks = comps // CHUNK
    counts = [tables[n].shape[0] for n in range(0, len(tables), chunks)]
    vmem = pl.BlockSpec(memory_space=pltpu.VMEM)
    return pl.pallas_call(
        functools.partial(score_kernel, first, counts, len(curvs), len(earlier)),
        in_specs=[vmem] * (4 + len(curvs) + len(earlier) + len(tables)),
        out_specs=vmem,
        out_shape=jax.ShapeDtypeStruct((1, comps + 128), F32)
        if curvs
        else pltpu.VMEM((C, comps), F32),
        scratch_shapes=[pltpu.VMEM((2, C, WIDE), BF16)],
        compiler_params=pltpu.CompilerParams(vmem_limit_bytes=SCOPED),
        cost_estimate=pl.CostEstimate(
            flops=2 * C * comps * sum(counts) * WIDE,
            bytes_accessed=2 * comps * sum(counts) * WIDE,
            transcendentals=0,
        ),
        name="scores",
    )(
        parts,
        observed,
        in_vmem(gain),
        clusters,
        *curvs,
        *map(in_vmem, earlier),
        *map(in_vmem, tables),
    )


def other_core():
    return [(i, i ^ 1) for i in range(32)]


def turn_y(k):
    return [(i, (i + 8 * k) % 32) for i in range(32)]


def turn_z(k):
    return [(i, i // 8 * 8 + ((i // 2 % 4 + k) % 4) * 2 + i % 2) for i in range(32)]


def plane_groups():
    return [[2 * i + core for i in range(16)] for core in range(2)]


def permute(x, pairs):
    return lax.ppermute(x, "row", pairs)


def per_device(
    baseline_uvw, sky_positions, fluxes, clusters, stations, station_gains, gain_step, observed_vis
):
    flux_row, cluster_row = fluxes[None, :], clusters[None, :]
    peers = lax.axis_size("comp")
    me = lax.axis_index("row").astype(jnp.int32)[None]
    firsts = [sum(GROUPS[:n]) for n in range(len(GROUPS))]

    owned = station_gains + gain_step
    others = [permute(owned, turn_z(k)) for k in (1, 2, 3)]
    groups, preds = [], []
    after = owned
    for n, count in enumerate(GROUPS):
        *group, pred, passed = make_tables(
            firsts[n],
            count,
            me,
            sky_positions,
            flux_row,
            cluster_row,
            baseline_uvw,
            after,
            after.shape[0] if n < 2 else 8,
            [x for held in groups for x in held] + preds,
        )
        groups.append(group)
        preds.append(pred)
        if n == 0:
            after = jnp.concatenate([passed] + others, axis=0)
            others = [permute(after, turn_y(k)) for k in (1, 2, 3)]
        elif n == 1:
            after = jnp.concatenate([passed] + others, axis=0)
            pieces = [after, permute(after, other_core())]

    tables = [x for held in groups for x in held]
    gains, curvs, sent = [], [], []
    for half in HALVES:
        gain, model, curv, *table = make_model(
            firsts[half[0]],
            me,
            pieces,
            stations,
            [preds[n] for n in half],
            tables + gains,
            peers,
        )
        gains.append(gain)
        curvs.append(curv)
        sent.append(lax.all_to_all(model, "comp", 0, 0, tiled=True))
        pieces = table
    earlier = []
    for n, half in enumerate(HALVES):
        sums = make_scores(
            firsts[half[0]],
            sent[n],
            observed_vis,
            gains[n],
            cluster_row,
            curvs if n == len(HALVES) - 1 else [],
            earlier,
            [x for group in half for x in groups[group]],
        )
        earlier = [sums]
    sums = sums + permute(sums, other_core())
    sums = lax.all_to_all(
        jnp.broadcast_to(sums[None], (16,) + sums.shape),
        "row",
        0,
        0,
        axis_index_groups=plane_groups(),
        tiled=True,
    )
    return pl.pallas_call(
        flux_kernel, out_shape=jax.ShapeDtypeStruct(flux_row.shape, F32), name="flux"
    )(sums, flux_row, cluster_row)[0]


def solution(mesh):
    return jax.shard_map(
        per_device,
        mesh=mesh,
        in_specs=(
            P(None, "row"),
            P(None, "comp"),
            P("comp"),
            P("comp"),
            P(None, "row"),
            P("row", None),
            P("row", None),
            P(None, None, "row"),
        ),
        out_specs=P("comp"),
        check_vma=False,
    )
```
